32 devices in a mesh: grp: 2 (over x), vocab: 8 (over z, y), row: 2 (over core).
Axes of the slice: x: 2, y: 2, z: 4, core: 2. Of those that a mesh axis runs over, the one named last changes fastest.
Arguments:
- hidden: bfloat16 [512, 2048], P(('grp', 'vocab'), 'row'), parts along dimension 0, may hold values from -160 to 160
- head_weight: bfloat16 [2048, 77824], P('row', 'vocab'), may hold values from -0.5 to 0.5
- teacher_ids: int32 [512, 32], P(('grp', 'row'), 'vocab'), parts along dimension 0, may hold values from 0 to 77823, as said below
- teacher_logprobs: float32 [512, 32], P(('grp', 'row'), 'vocab'), parts along dimension 0, may hold values from -14 to -0.5
- valid: int32 [512], P(('grp', 'row')), parts along dimension 0, may hold values 0 or 1
- row_weight: float32 [512], P(('grp', 'row')), parts along dimension 0, may hold values from 16384 to 131072
Outputs:
- hidden_grad: bfloat16 [512, 2048], P(('grp', 'vocab'), 'row'), parts along dimension 0
- weight_grad: bfloat16 [4096, 77824], P(('grp', 'row'), 'vocab'), parts along dimension 0
The draws below stay inside these ranges and needn't reach their ends.
There are 2 independent parts, one for each index of `grp`. The reference program is written for one: setup_inputs(seed, part) draws one part's arguments, and reference() takes and returns one part's arrays. A program takes and returns all parts, laid end to end along the dimension named above; an argument that names none is the same for every part. Nothing has to cross between parts.
Inputs may be any that keep to these rules, and one draw needn't show every extreme that they name: `teacher_ids`: the 32 ids of a row are distinct.
All inputs are finite; a program needn't handle non-finite values. No bound on the sum of `valid` on one device may be relied on, other than what follows from the above.
Results may differ from the reference program's by a relative error of at most 0.0055.
Values may be sent and summed in bfloat16 or wider, within the bound.
No kernel may reach another device: no remote copies, remote signals or barrier semaphores. Data moves between devices by JAX's collectives and lax.ppermute only.
A program may use at most 192 MiB of HBM per device.

```python
import math
import jax
import jax.numpy as jnp
from jax import lax

R = 256
D = 2048
V = 77824
K = 32


def draw_hidden(key, part):
    key = jax.random.fold_in(key, 5)
    first = jax.random.fold_in(key, 0)
    values = jnp.clip(jax.random.normal(first, (R, D), jnp.float32), -6.0, 6.0)
    return values.astype(jnp.bfloat16)


def draw_head_weight(key, part):
    key = jax.random.fold_in(key, 17)
    first, second = jax.random.split(key)
    base = jnp.clip(jax.random.normal(first, (D, V), jnp.float32), -2.5, 2.5)
    scale = jnp.exp(jax.random.uniform(second, (1, V), jnp.float32, math.log(0.6), math.log(1.6)))
    values = base * scale * (1.0 / math.sqrt(D))
    return values.astype(jnp.bfloat16)


def draw_teacher_ids(key, part):
    key = jax.random.fold_in(key, 11)
    room = (2 ** 31 - 1) // V
    scores = jax.random.randint(key, (R, V), 0, room, dtype=jnp.int32) * V + jnp.arange(V, dtype=jnp.int32)[None, :]
    rows = jnp.arange(R, dtype=jnp.int32)[:, None]
    columns = jnp.arange(V, dtype=jnp.int32)[None, :]
    forced = (rows == 0) & (columns == V - 1) | (rows == 1) & (columns == 0)
    scores = jnp.where(forced, jnp.int32(2 ** 31 - 1), scores)
    chosen = lax_top(scores)
    return chosen.astype(jnp.int32)


def lax_top(scores):
    values, indices = jax.lax.top_k(scores, K)
    return indices


def with_ends(entries, key, smallest, high):
    index_at = [jax.random.randint(jax.random.fold_in(key, axis), (), 0, length) for axis, length in enumerate(entries.shape)]
    main_axis = entries.shape.index(max(entries.shape))
    beside = index_at[:main_axis] + [(index_at[main_axis] + 1) % entries.shape[main_axis]] + index_at[main_axis + 1:]
    return entries.at[tuple(index_at)].set(smallest).at[tuple(beside)].set(high)


def steps_of(stream_key, shape, shards, smallest, high):
    def one(axis_at, blocks):
        heights = jax.random.uniform(jax.random.fold_in(jax.random.fold_in(stream_key, 6), axis_at), (blocks,), jnp.float32, smallest / len(shards), high / len(shards))
        return jnp.repeat(jnp.exp(heights), shape[axis_at] // blocks).reshape((-1,) + (1,) * (len(shape) - axis_at - 1))

    factor_of = one(*shards[0])
    for cut in shards[1:]:
        factor_of = factor_of * one(*cut)
    return factor_of


def setup_inputs(seed: int = 0, part: int = 0) -> dict:
    key_of = jax.random.split(jax.random.key(seed), 7)
    own_keys = jax.random.split(jax.random.fold_in(key_of[6], part), 7)
    return {
        "hidden": draw_hidden(jax.random.fold_in(jax.random.fold_in(key_of[6], part), 71), part),
        "head_weight": draw_head_weight(jax.random.fold_in(key_of[6], 71), part),
        "teacher_ids": draw_teacher_ids(jax.random.fold_in(jax.random.fold_in(key_of[6], part), 71), part),
        "teacher_logprobs": jnp.clip(-14.0 + 13.5 * jax.random.uniform(own_keys[3], (R, K), jnp.float32) ** steps_of(own_keys[3], (R, K), ((0, 2), (1, 8)), -0.2, 0.2), -14.0, -0.5),
        "valid": with_ends((jax.random.randint(own_keys[4], (R,), 0, 4) < 3).astype(jnp.int32), jax.random.fold_in(own_keys[4], 1), 0, 1),
        "row_weight": jnp.clip(jnp.exp(math.log(131072.0) - 2.0794415 * jax.random.uniform(own_keys[5], (R,), jnp.float32) ** steps_of(own_keys[5], (R,), ((0, 2),), -0.2, 0.2)), 16384.0, 131072.0),
    }


def reference(hidden, head_weight, teacher_ids, teacher_logprobs, valid, row_weight):
    logits = jnp.dot(hidden, head_weight, preferred_element_type=jnp.float32)
    top = jnp.max(logits, axis=1)
    lse = top + jnp.log(jnp.sum(jnp.exp(logits - top[:, None]), axis=1))
    support = jnp.take_along_axis(logits, teacher_ids, axis=1) - lse[:, None]
    scale_rows = row_weight * valid.astype(jnp.float32)
    support_grad = scale_rows[:, None] * jnp.exp(support) * (support - teacher_logprobs + 1.0)
    total = jnp.sum(support_grad, axis=1)
    dense = -jnp.exp(logits - lse[:, None]) * total[:, None]
    row_index = jnp.broadcast_to(jnp.arange(logits.shape[0], dtype=jnp.int32)[:, None], teacher_ids.shape)
    dense = dense.at[row_index, teacher_ids].add(support_grad)
    logit_grad = dense.astype(jnp.bfloat16)
    hidden_grad = lax.dot_general(logit_grad, head_weight, (((1,), (1,)), ((), ())), preferred_element_type=jnp.float32)
    weight_grad = lax.dot_general(hidden, logit_grad, (((0,), (0,)), ((), ())), preferred_element_type=jnp.float32)
    return hidden_grad.astype(jnp.bfloat16), weight_grad.astype(jnp.bfloat16)
```

```python
import functools

import jax
import jax.numpy as jnp
from jax import lax
from jax.experimental import pallas as pl
from jax.experimental.pallas import tpu as pltpu
from jax.sharding import PartitionSpec as P

VMEM_LIMIT = 48 * 1024 * 1024
TILE = 8
STEP = 16
NT = (((1,), (1,)), ((), ()))
F32 = jnp.float32
BF16 = jnp.bfloat16


def _params():
    return pltpu.CompilerParams(vmem_limit_bytes=VMEM_LIMIT)


def _cost(flops, nbytes):
    return pl.CostEstimate(flops=int(flops), bytes_accessed=int(nbytes), transcendentals=0)


def _split(width):
    unit = 256 if width % 256 == 0 else 128
    units = width // unit
    first = (units + 1) // 2
    first += first % 2 if units > 4 else 0
    out = []
    start = 0
    for count in (first, units - first):
        if count:
            best = max(d for d in range(1, count + 1) if count % d == 0 and d * unit <= 1536)
            out.append((start * unit, count * unit, best * unit))
            start += count
    return out


def _xor(n, s):
    return [(i, i ^ s) for i in range(n)]


def _w_spec(depth, chunk):
    start, _, block = chunk
    return pl.BlockSpec(
        (pl.Element(depth), pl.Element(block)),
        lambda j: (0, pl.multiple_of(start + j * block, 128)),
    )


def _whole(shape):
    return pl.BlockSpec(shape, lambda j: (0,) * len(shape))


def _logits_body(h_ref, w_ref, own_ref, send_ref):
    part = jnp.dot(h_ref[...], w_ref[...], preferred_element_type=F32)
    half = own_ref.shape[0]
    own_ref[...] = part[:half]
    send_ref[...] = part[half:]


def _partial_logits(h, w, chunk):
    _, width, block = chunk
    rows, depth = h.shape
    half = rows // 2
    out = jax.ShapeDtypeStruct((half, width), F32)
    spec = pl.BlockSpec((half, block), lambda j: (0, j))
    return pl.pallas_call(
        _logits_body,
        grid=(width // block,),
        in_specs=[_whole((rows, depth)), _w_spec(depth, chunk)],
        out_specs=[spec, spec],
        out_shape=[out, out],
        compiler_params=_params(),
        cost_estimate=_cost(2 * rows * depth * width, 2 * depth * width + 4 * rows * width),
        name="partial_logits",
    )(h, w)


def _row_mask(lanes, terms):
    lane_row = lax.broadcasted_iota(jnp.int32, (TILE, lanes), 1) // terms
    return lane_row == lax.broadcasted_iota(jnp.int32, (TILE, lanes), 0)


def _exp_body(start, last, *refs):
    if last:
        own_ref, recv_ref, ids_ref, lps_ref, picks_in, stat_in, e_ref, picks_ref, stat_ref, tot_ref, hold = refs
    else:
        own_ref, recv_ref, ids_ref, e_ref, picks_ref, stat_ref = refs
    step = pl.program_id(0)
    width = own_ref.shape[1]
    lanes = ids_ref.shape[1]
    terms = lanes // TILE
    mask = _row_mask(lanes, terms)
    lane = lax.broadcasted_iota(jnp.int32, (TILE, 128), 1)
    for t in range(STEP // TILE):
        tile = step * (STEP // TILE) + t
        rows = slice(t * TILE, (t + 1) * TILE)
        rel = jnp.broadcast_to(ids_ref[pl.ds(tile, 1), :] - start, (TILE, lanes))
        key = jnp.where(mask, rel >> 7, -1)
        slot = rel & 127
        groups = range(lanes // 128)
        slots = [slot[:, g * 128 : (g + 1) * 128] for g in groups]
        keys = [key[:, g * 128 : (g + 1) * 128] for g in groups]
        acc = [jnp.zeros((TILE, 128), F32) for _ in groups]
        top = jnp.full((TILE, 128), -jnp.inf, F32)
        for c in range(width // 128):
            cols = slice(c * 128, (c + 1) * 128)
            logit = own_ref[rows, cols] + recv_ref[rows, cols]
            e_ref[rows, cols] = logit
            top = jnp.maximum(top, logit)
            for g in groups:
                got = jnp.take_along_axis(logit, slots[g], axis=1, mode="promise_in_bounds")
                acc[g] = jnp.where(keys[g] == c, got, acc[g])
        top = jnp.max(top, axis=1, keepdims=True)
        total = jnp.zeros((TILE, 128), F32)
        for c in range(width // 128):
            cols = slice(c * 128, (c + 1) * 128)
            e = jnp.exp(e_ref[rows, cols] - top)
            e_ref[rows, cols] = e
            total = total + e
        total = jnp.sum(total, axis=1, keepdims=True)
        picked = jnp.concatenate(acc, axis=1)
        if last:
            picked = picked + picks_in[rows, :]
        picks_ref[rows, :] = picked
        stat_ref[rows, :] = jnp.where(lane == 0, top, total)
        if last:
            before = stat_in[rows, :]
            top0, total0 = before[:, 0:1], before[:, 1:2]
            both = jnp.maximum(top, top0)
            total = total * jnp.exp(top - both) + total0 * jnp.exp(top0 - both)
            whole = jnp.broadcast_to(ids_ref[pl.ds(tile, 1), :], (TILE, lanes))
            inside = mask & (whole >= 0) & (whole < start + width)
            weight = jnp.where(inside, jnp.exp(picked - both), 0.0)
            teacher = jnp.broadcast_to(lps_ref[pl.ds(tile, 1), :], (TILE, lanes))
            first = jnp.sum(weight * (picked - both - teacher + 1.0), axis=1, keepdims=True)
            plain = jnp.sum(weight, axis=1, keepdims=True)
            hold[pl.ds(tile * TILE, TILE), :] = jnp.where(
                lane == 0, both, jnp.where(lane == 1, total, jnp.where(lane == 2, first, plain))
            )
    if last:

        @pl.when(step == pl.num_programs(0) - 1)
        def _():
            tot_ref[...] = hold[...].T[:TILE, :]


def _exponentials(own, recv, ids, chunk, lps=None, before=None):
    start, width, _ = chunk
    half = own.shape[0]
    tiles, lanes = ids.shape
    last = before is not None
    row = lambda w: pl.BlockSpec((STEP, w), lambda i: (i, 0))
    out_shape = [
        jax.ShapeDtypeStruct((half, width), F32),
        jax.ShapeDtypeStruct((half, lanes), F32),
        jax.ShapeDtypeStruct((half, 128), F32),
    ]
    out_specs = [row(width), row(lanes), row(128)]
    in_specs = [row(width), row(width), _whole((tiles, lanes))]
    args = [own, recv, ids]
    scratch = []
    if last:
        in_specs += [_whole((tiles, lanes)), row(lanes), row(128)]
        args += [lps, *before]
        out_shape.append(jax.ShapeDtypeStruct((TILE, half), F32))
        out_specs.append(_whole((TILE, half)))
        scratch = [pltpu.VMEM((half, 128), F32)]
    return pl.pallas_call(
        functools.partial(_exp_body, start, last),
        grid=(half // STEP,),
        in_specs=in_specs,
        out_specs=out_specs,
        out_shape=out_shape,
        scratch_shapes=scratch,
        compiler_params=_params(),
        cost_estimate=_cost(8 * half * width, 12 * half * width),
        name="exponentials",
    )(*args)


def _join_stats(a, b):
    top = jnp.maximum(a[0], b[0])
    da, db = a[0] - top, b[0] - top
    fa, fb = jnp.exp(da), jnp.exp(db)
    return jnp.stack(
        [
            top,
            a[1] * fa + b[1] * fb,
            (a[2] + da * a[3]) * fa + (b[2] + db * b[3]) * fb,
            a[3] * fa + b[3] * fb,
        ]
    )


def _grad_body(start, e_ref, stat_ref, picks_ref, ids_ref, lps_ref, tot_ref, g_ref, hold):
    step = pl.program_id(0)
    width = e_ref.shape[1]
    lanes = ids_ref.shape[1]
    terms = lanes // TILE
    half = tot_ref.shape[1]

    @pl.when(step == 0)
    def _():
        hold[...] = jnp.concatenate([tot_ref[...], jnp.zeros((128 - TILE, half), F32)], axis=0).T

    mask = _row_mask(lanes, terms)
    parts = (width + 255) // 256
    place = lax.broadcasted_iota(jnp.int32, (256, lanes), 0)
    coefs, terms_of = [], []
    for t in range(STEP // TILE):
        tile = step * (STEP // TILE) + t
        rows = slice(t * TILE, (t + 1) * TILE)
        tot = hold[pl.ds(tile * TILE, TILE), :]
        top, total, first, plain, scale = (tot[:, i : i + 1] for i in range(5))
        log_sum = jnp.log(total)
        lse = top + log_sum
        sum_grad = scale * jnp.exp(-log_sum) * (first - log_sum * plain)
        coefs.append(sum_grad * jnp.exp(stat_ref[rows, 0:1] - lse))
        rel_row = ids_ref[pl.ds(tile, 1), :] - start
        rel = jnp.broadcast_to(rel_row, (TILE, lanes))
        inside = mask & (rel >= 0) & (rel < width)
        support = picks_ref[rows, :] - lse
        grad = scale * jnp.exp(support) * (support - lps_ref[pl.ds(tile, 1), :] + 1.0)
        grad = jnp.where(inside, grad, 0.0)
        high = grad.astype(BF16).astype(F32)
        low = grad - high
        key = jnp.where(inside, rel >> 8, -1)
        lhs = jnp.concatenate(
            [
                jnp.concatenate([jnp.where(key == c, high, 0.0), jnp.where(key == c, low, 0.0)], axis=1)
                for c in range(parts)
            ],
            axis=0,
        ).astype(BF16)
        hot = (place == jnp.broadcast_to(rel_row & 255, (256, lanes))).astype(F32).astype(BF16)
        rhs = jnp.concatenate([hot, hot], axis=1)
        terms_of.append(lax.dot_general(lhs, rhs, NT, preferred_element_type=F32))
    for c in range(parts):
        size = min(256, width - c * 256)
        cols = slice(c * 256, c * 256 + size)
        out = [
            terms_of[t][c * TILE : (c + 1) * TILE, :size] - e_ref[t * TILE : (t + 1) * TILE, cols] * coefs[t]
            for t in range(STEP // TILE)
        ]
        g_ref[:, cols] = jnp.concatenate(out, axis=0).astype(BF16)


def _logit_grad(e, stat, picks, ids, lps, tot, chunk):
    start, width, _ = chunk
    half = e.shape[0]
    tiles, lanes = ids.shape
    row = lambda w: pl.BlockSpec((STEP, w), lambda i: (i, 0))
    return pl.pallas_call(
        functools.partial(_grad_body, start),
        grid=(half // STEP,),
        in_specs=[row(width), row(128), row(lanes), _whole((tiles, lanes)), _whole((tiles, lanes)), _whole(tot.shape)],
        out_specs=row(width),
        out_shape=jax.ShapeDtypeStruct((half, width), BF16),
        scratch_shapes=[pltpu.VMEM((half, 128), F32)],
        compiler_params=_params(),
        cost_estimate=_cost(8 * half * width, 6 * half * width),
        name="logit_grad",
    )(e, stat, picks, ids, lps, tot)


def _feature_body(last, count, *refs):
    if last:
        order_ref, own_ref, other_ref, w_ref, before_ref, keep_ref, send_ref, acc = refs
    else:
        own_ref, other_ref, w_ref, acc = refs
    step = pl.program_id(0)
    grads = jnp.concatenate([own_ref[...], other_ref[...]], axis=0)
    part = lax.dot_general(grads, w_ref[...], NT, preferred_element_type=F32)

    @pl.when(step == 0)
    def _():
        acc[...] = part + before_ref[...] if last else part

    @pl.when(step > 0)
    def _():
        acc[...] += part

    if last:

        @pl.when(step == pl.num_programs(0) - 1)
        def _():
            rows = acc.shape[0] // count
            near, far = [], []
            for d in range(count):
                at = pl.multiple_of(order_ref[d] * rows, rows)
                (far if d % 2 else near).append(acc[pl.ds(at, rows), :])
            keep_ref[...] = jnp.concatenate(near, axis=0)
            send_ref[...] = jnp.concatenate(far, axis=0).astype(BF16)


def _feature_terms(own, other, w, chunk, order=None, before=None):
    _, width, block = chunk
    half = own.shape[0]
    depth = w.shape[0]
    last = before is not None
    part = pl.BlockSpec((half, block), lambda j: (0, j))
    in_specs = [part, part, _w_spec(depth, chunk)]
    args = [own, other, w]
    if last:
        in_specs = [pl.BlockSpec(memory_space=pltpu.SMEM)] + in_specs + [_whole((2 * half, depth))]
        args = [order] + args + [before]
        out_shape = [jax.ShapeDtypeStruct((half, depth), F32), jax.ShapeDtypeStruct((half, depth), BF16)]
        out_specs = [_whole((half, depth))] * 2
        scratch = [pltpu.VMEM((2 * half, depth), F32)]
    else:
        out_shape = jax.ShapeDtypeStruct((2 * half, depth), F32)
        out_specs = _whole((2 * half, depth))
        scratch = []
    return pl.pallas_call(
        functools.partial(_feature_body, last, order.shape[0] if last else 0),
        grid=(width // block,),
        in_specs=in_specs,
        out_specs=out_specs,
        out_shape=out_shape,
        scratch_shapes=scratch,
        compiler_params=_params(),
        cost_estimate=_cost(4 * half * depth * width, 2 * depth * width + 4 * half * width),
        name="feature_terms",
    )(*args)


def _weight_body(ht_ref, own_ref, other_ref, *refs):
    grads = jnp.concatenate([own_ref[...], other_ref[...]], axis=0)
    refs[-1][...] = jnp.dot(ht_ref[...], grads, preferred_element_type=F32).astype(BF16)


def _weight_grad(ht, own, other, chunk, width_all, before=None):
    _, width, block = chunk
    depth, rows = ht.shape
    part = pl.BlockSpec((rows // 2, block), lambda j: (0, j))
    in_specs = [_whole((depth, rows)), part, part]
    args = [ht, own, other]
    aliases = {}
    if before is not None:
        in_specs.append(pl.BlockSpec(memory_space=pl.ANY))
        args.append(before)
        aliases = {3: 0}
    return pl.pallas_call(
        _weight_body,
        grid=(width // block,),
        in_specs=in_specs,
        out_specs=_w_spec(depth, chunk),
        out_shape=jax.ShapeDtypeStruct((depth, width_all), BF16),
        input_output_aliases=aliases,
        compiler_params=_params(),
        cost_estimate=_cost(2 * rows * depth * width, 2 * depth * width + 2 * rows * width),
        name="weight_grad",
    )(*args)


def per_device(hidden, head_weight, teacher_ids, teacher_logprobs, valid, row_weight):
    count = lax.axis_size("vocab")
    bits = count.bit_length() - 1
    r = lax.axis_index("row")
    v = lax.axis_index("vocab")
    depth, width = head_weight.shape
    half = teacher_ids.shape[0]
    swap = [(0, 1), (1, 0)]
    chunks = _split(width)

    h = hidden[None]
    for b in reversed(range(bits)):
        far = lax.ppermute(h, "vocab", _xor(count, 1 << b))
        bit = (v >> b) & 1
        first = bit == r if b == bits - 1 else bit == 0
        h = jnp.stack([jnp.where(first, h, far), jnp.where(first, far, h)], axis=1)
        h = h.reshape((-1,) + hidden.shape)
    h = h.reshape(-1, hidden.shape[1])
    ht = h.T

    own_terms = teacher_ids.shape[1]
    packed = jnp.concatenate([teacher_ids.astype(F32).T, teacher_logprobs.T], axis=0)
    packed = packed.reshape(1, 2, own_terms, half)
    for b in range(bits):
        packed = jnp.concatenate([packed, lax.ppermute(packed, "vocab", _xor(count, 1 << b))], axis=0)
    flat = packed.transpose(1, 3, 0, 2).reshape(2, half // TILE, -1)
    ids = flat[0].astype(jnp.int32) - v * width
    lps = flat[1]

    parts = []
    for chunk in chunks:
        own, send = _partial_logits(h, head_weight, chunk)
        parts.append((own, lax.ppermute(send, "row", swap)))
    e0, picks, stat0 = _exponentials(*parts[0], ids, chunks[0])
    e1, picks, stat1, stats = _exponentials(*parts[1], ids, chunks[1], lps, (picks, stat0))

    stats = stats[:4]
    for b in range(bits):
        stats = _join_stats(stats, lax.ppermute(stats, "vocab", _xor(count, 1 << b)))
    scale = row_weight * valid.astype(F32)
    tot = jnp.concatenate([stats, scale[None], jnp.zeros((3, half), F32)], axis=0)

    grads = []
    for chunk, e, stat in zip(chunks, (e0, e1), (stat0, stat1)):
        own = _logit_grad(e, stat, picks, ids, lps, tot, chunk)
        grads.append((own, lax.ppermute(own, "row", swap)))

    top_bit = count // 2
    order = (jnp.arange(count, dtype=jnp.int32) ^ v) ^ (r * top_bit)
    terms = _feature_terms(*grads[0], head_weight, chunks[0])
    keep, send = _feature_terms(*grads[1], head_weight, chunks[1], order, terms)

    keep = keep + lax.ppermute(send, "vocab", _xor(count, 1)).astype(F32)
    keep = keep.reshape((count // 2,) + hidden.shape)
    total = keep[0]
    for d in range(1, count // 2):
        far = lax.ppermute(keep[d].astype(BF16), "vocab", _xor(count, 2 * d))
        total = total + far.astype(F32)
    hidden_grad = total.astype(BF16)

    weight_grad = _weight_grad(ht, *grads[0], chunks[0], width)
    weight_grad = _weight_grad(ht, *grads[1], chunks[1], width, weight_grad)
    return hidden_grad, weight_grad


def solution(mesh):
    return jax.shard_map(
        per_device,
        mesh=mesh,
        in_specs=(
            P(("grp", "vocab"), "row"),
            P("row", "vocab"),
            P(("grp", "row"), "vocab"),
            P(("grp", "row"), "vocab"),
            P(("grp", "row")),
            P(("grp", "row")),
        ),
        out_specs=(P(("grp", "vocab"), "row"), P(("grp", "row"), "vocab")),
        check_vma=False,
    )
```

```python
import functools

import jax
import jax.numpy as jnp
from jax import lax
from jax.experimental import pallas as pl
from jax.experimental.pallas import tpu as pltpu
from jax.sharding import PartitionSpec as P

VMEM_LIMIT = 14 * 1024 * 1024
TILE = 8
STEP = 16
NT = (((1,), (1,)), ((), ()))
F32 = jnp.float32
BF16 = jnp.bfloat16
LOCAL = pl.BlockSpec(memory_space=pltpu.VMEM)
WRITES = 4


def _local(x):
    return pltpu.with_memory_space_constraint(x, pltpu.VMEM)


def _cost(flops, nbytes):
    return pl.CostEstimate(flops=int(flops), bytes_accessed=int(nbytes), transcendentals=0)


def _call(body, name, args, out_shape, cost, specs=None, out_specs=None, scratch=(), aliases=None):
    specs = specs or [LOCAL] * len(args)
    args = [_local(x) if s is LOCAL else x for x, s in zip(args, specs)]
    return pl.pallas_call(
        body,
        in_specs=specs,
        out_specs=out_specs or [LOCAL] * len(out_shape),
        out_shape=out_shape,
        scratch_shapes=list(scratch),
        input_output_aliases=aliases or {},
        compiler_params=pltpu.CompilerParams(vmem_limit_bytes=VMEM_LIMIT),
        cost_estimate=cost,
        name=name,
    )(*args)


def _split(width, count):
    unit = 256 if width % 256 == 0 else 128
    units = width // unit
    ends = [units * (i + 1) // count for i in range(count)]
    starts = [0] + ends[:-1]
    return [(a * unit, (b - a) * unit) for a, b in zip(starts, ends)]


def _blocks(width, block):
    return [(a, min(block, width - a)) for a in range(0, width, block)]


def _xor(n, s):
    return [(i, i ^ s) for i in range(n)]


def _logits_body(start, h_ref, w_ref, own_ref, send_ref):
    half = own_ref.shape[0]
    for at, size in _blocks(own_ref.shape[1], 1280):
        part = jnp.dot(h_ref[...], w_ref[:, start + at : start + at + size], preferred_element_type=F32)
        own_ref[:, at : at + size] = part[:half]
        send_ref[:, at : at + size] = part[half:]


def _partial_logits(h, w, chunk):
    start, width = chunk
    rows, depth = h.shape
    out = pltpu.VMEM((rows // 2, width), F32)
    return _call(
        functools.partial(_logits_body, start),
        "partial_logits",
        [h, w],
        [out, out],
        _cost(2 * rows * depth * width, 2 * depth * width + 4 * rows * width),
    )


def _exp_body(start, width, index, count, terms, *refs):
    first, last = index == 0, index == count - 1
    refs = list(refs)
    own_ref, recv_ref = refs.pop(0), refs.pop(0)
    if first:
        packed_ref = refs.pop(0)
    else:
        ids_ref, lps_ref, picks_in = refs.pop(0), refs.pop(0), refs.pop(0)
    before = [refs.pop(0) for _ in range(index)] if last else []
    e_ref, picks_ref, stat_ref = refs.pop(0), refs.pop(0), refs.pop(0)
    half = own_ref.shape[0]
    if first:
        ids_ref, lps_ref = refs.pop(0), refs.pop(0)
        pad = jnp.full((128 - terms, half), -1.0, F32)
        ids_ref[...] = jnp.concatenate([packed_ref[0], pad], axis=0).T.astype(jnp.int32)
        lps_ref[...] = jnp.concatenate([packed_ref[1], pad], axis=0).T
    if last:
        tot_ref, hold = refs
    lane = lax.broadcasted_iota(jnp.int32, (TILE, 128), 1)
    ways = 4

    def tile(t, carry):
        rows = pl.ds(pl.multiple_of(t * TILE, TILE), TILE)
        ids = ids_ref[rows, :]
        rel = ids - start
        key = rel >> 7
        slot = rel & 127
        acc = [jnp.zeros((TILE, 128), F32)] * ways
        top = [jnp.full((TILE, 128), -jnp.inf, F32)] * ways
        for c in range(width // 128):
            cols = slice(c * 128, (c + 1) * 128)
            w = c % ways
            logit = own_ref[rows, cols] + recv_ref[rows, cols]
            e_ref[rows, cols] = logit
            top[w] = jnp.maximum(top[w], logit)
            got = jnp.take_along_axis(logit, slot, axis=1, mode="promise_in_bounds")
            acc[w] = jnp.where(key == c, got, acc[w])
        top = functools.reduce(jnp.maximum, top)
        top = jnp.max(top, axis=1, keepdims=True)
        total = [jnp.zeros((TILE, 128), F32)] * ways
        for c in range(width // 128):
            cols = slice(c * 128, (c + 1) * 128)
            e = jnp.exp(e_ref[rows, cols] - top)
            e_ref[rows, cols] = e
            total[c % ways] += e
        total = jnp.sum(sum(total), axis=1, keepdims=True)
        picked = sum(acc)
        if not first:
            picked = picked + picks_in[rows, :]
        picks_ref[rows, :] = picked
        stat_ref[rows, :] = jnp.where(lane == 0, top, total)
        if last:
            tops, totals = [top], [total]
            for ref in before:
                tops.append(ref[rows, 0:1])
                totals.append(ref[rows, 1:2])
            both = functools.reduce(jnp.maximum, tops)
            total = sum(s * jnp.exp(m - both) for m, s in zip(tops, totals))
            inside = (ids >= 0) & (ids < start + width)
            weight = jnp.where(inside, jnp.exp(picked - both), 0.0)
            mixed = jnp.sum(weight * (picked - both - lps_ref[rows, :] + 1.0), axis=1, keepdims=True)
            plain = jnp.sum(weight, axis=1, keepdims=True)
            hold[rows, :] = jnp.where(
                lane == 0, both, jnp.where(lane == 1, total, jnp.where(lane == 2, mixed, plain))
            )
        return carry

    lax.fori_loop(0, half // TILE, tile, 0, unroll=2)
    if last:
        tot_ref[...] = hold[...].T[:TILE, :]


def _exponentials(own, recv, chunks, index, terms, packed=None, rows=None, picks=None, before=()):
    start, width = chunks[index]
    half = own.shape[0]
    first, last = index == 0, index == len(chunks) - 1
    table = pltpu.VMEM((half, 128), F32)
    args = [own, recv] + ([packed] if first else [*rows, picks]) + (list(before) if last else [])
    out = [pltpu.VMEM((half, width), F32), table, table]
    scratch = []
    if first:
        out += [pltpu.VMEM((half, 128), jnp.int32), table]
    if last:
        out.append(pltpu.VMEM((TILE, half), F32))
        scratch = [pltpu.VMEM((half, 128), F32)]
    return _call(
        functools.partial(_exp_body, start, width, index, len(chunks), terms),
        "exponentials",
        args,
        out,
        _cost(8 * half * width, 12 * half * width),
        scratch=scratch,
    )


def _join_stats(a, b):
    top = jnp.maximum(a[0], b[0])
    da, db = a[0] - top, b[0] - top
    fa, fb = jnp.exp(da), jnp.exp(db)
    return jnp.stack(
        [
            top,
            a[1] * fa + b[1] * fb,
            (a[2] + da * a[3]) * fa + (b[2] + db * b[3]) * fb,
            a[3] * fa + b[3] * fb,
        ]
    )


def _grad_body(chunks, terms, *refs):
    count = len(chunks)
    e_refs, stat_refs = refs[:count], refs[count : 2 * count]
    picks_ref, ids_ref, lps_ref, tot_ref, g_ref, hold = refs[2 * count :]
    half = tot_ref.shape[1]
    lanes = TILE * terms
    hold[...] = jnp.concatenate([tot_ref[...], jnp.zeros((128 - TILE, half), F32)], axis=0).T
    lane_row = lax.broadcasted_iota(jnp.int32, (TILE, lanes), 1) // terms
    mask = lane_row == lax.broadcasted_iota(jnp.int32, (TILE, lanes), 0)
    place = lax.broadcasted_iota(jnp.int32, (256, lanes), 0)
    begin = chunks[0][0]
    width = sum(w for _, w in chunks)
    parts = (width + 255) // 256

    def flat(x):
        return jnp.concatenate([x[:, :terms]] * TILE, axis=1)

    def tile(t):
        rows = pl.ds(pl.multiple_of(t * TILE, TILE), TILE)
        tot = hold[rows, :]
        top, total, mixed, plain, scale = (tot[:, i : i + 1] for i in range(5))
        log_sum = jnp.log(total)
        lse = top + log_sum
        sum_grad = scale * jnp.exp(-log_sum) * (mixed - log_sum * plain)
        coefs = [sum_grad * jnp.exp(ref[rows, 0:1] - lse) for ref in stat_refs]
        rel = ids_ref[rows, :] - begin
        inside = (rel >= 0) & (rel < width)
        support = picks_ref[rows, :] - lse
        grad = scale * jnp.exp(support) * (support - lps_ref[rows, :] + 1.0)
        grad = jnp.where(inside, grad, 0.0)
        high = grad.astype(BF16).astype(F32)
        key = jnp.where(mask, flat(jnp.where(inside, rel >> 8, -1)), -1)
        col = jnp.where(mask, flat(rel & 255), 0)
        col = jnp.sum(col, axis=0, keepdims=True)
        high, low = flat(high), flat(grad - high)
        lhs = jnp.concatenate(
            [
                jnp.concatenate([jnp.where(key == c, high, 0.0), jnp.where(key == c, low, 0.0)], axis=1)
                for c in range(parts)
            ],
            axis=0,
        ).astype(BF16)
        hot = (place == jnp.broadcast_to(col, (256, lanes))).astype(F32).astype(BF16)
        rhs = jnp.concatenate([hot, hot], axis=1)
        return rows, coefs, lax.dot_general(lhs, rhs, NT, preferred_element_type=F32)

    def step(i, carry):
        pair = [tile(i * (STEP // TILE) + t) for t in range(STEP // TILE)]
        out_rows = pl.ds(pl.multiple_of(i * STEP, STEP), STEP)
        for q, (start, w) in enumerate(chunks):
            for at, size in _blocks(w, 128):
                col = start - begin + at
                c, off = col // 256, col % 256
                out = [
                    s[c * TILE : (c + 1) * TILE, off : off + size] - e_refs[q][rows, at : at + size] * coefs[q]
                    for rows, coefs, s in pair
                ]
                g_ref[out_rows, col : col + size] = jnp.concatenate(out, axis=0).astype(BF16)
        return carry

    lax.fori_loop(0, half // STEP, step, 0)


def _logit_grad(es, stats, picks, ids, lps, tot, chunks, terms):
    half = es[0].shape[0]
    width = sum(w for _, w in chunks)
    return _call(
        functools.partial(_grad_body, chunks, terms),
        "logit_grad",
        [*es, *stats, picks, ids, lps, tot],
        [pltpu.VMEM((half, width), BF16)],
        _cost(8 * half * width, 6 * half * width),
        scratch=[pltpu.VMEM((half, 128), F32)],
    )[0]


def _feature_body(start, count, *refs):
    if count:
        own_ref, other_ref, w_ref, before_ref, order_ref, keep_ref, send_ref, acc = refs
    else:
        own_ref, other_ref, w_ref, acc = refs
    width = own_ref.shape[1]
    grads = jnp.concatenate([own_ref[...], other_ref[...]], axis=0)
    part = lax.dot_general(grads, w_ref[:, start : start + width], NT, preferred_element_type=F32)
    if not count:
        acc[...] = part
        return
    acc[...] = part + before_ref[...]
    rows = acc.shape[0] // count
    near, far = [], []
    for d in range(count):
        at = pl.multiple_of(order_ref[d] * rows, rows)
        (far if d % 2 else near).append(acc[pl.ds(at, rows), :])
    keep_ref[...] = jnp.concatenate(near, axis=0)
    send_ref[...] = jnp.concatenate(far, axis=0).astype(BF16)


def _feature_terms(own, other, w, start, before=None, order=None):
    half, width = own.shape
    depth = w.shape[0]
    args = [own, other, w]
    specs = [LOCAL] * 3
    scratch = []
    out = [pltpu.VMEM((2 * half, depth), F32)]
    if before is not None:
        args += [before, order]
        specs += [LOCAL, pl.BlockSpec(memory_space=pltpu.SMEM)]
        scratch = out
        out = [pltpu.VMEM((half, depth), F32), pltpu.VMEM((half, depth), BF16)]
    return _call(
        functools.partial(_feature_body, start, 0 if before is None else order.shape[0]),
        "feature_terms",
        args,
        out,
        _cost(4 * half * depth * width, 2 * depth * width + 4 * half * width),
        specs=specs,
        scratch=scratch,
    )


def _weight_body(start, block, ht_ref, own_ref, other_ref, *refs):
    out_ref, ring, sems = refs[-3:]
    copies = []
    for i, (at, size) in enumerate(_blocks(own_ref.shape[1], block)):
        slot = i % WRITES
        if i >= WRITES:
            copies[i - WRITES].wait()
        cols = slice(at, at + size)
        grads = jnp.concatenate([own_ref[:, cols], other_ref[:, cols]], axis=0)
        ring[slot, :, :size] = jnp.dot(ht_ref[...], grads, preferred_element_type=F32).astype(BF16)
        copy = pltpu.make_async_copy(
            ring.at[slot, :, pl.ds(0, size)], out_ref.at[:, pl.ds(start + at, size)], sems.at[slot]
        )
        copy.start()
        copies.append(copy)
    for copy in copies[-WRITES:]:
        copy.wait()


def _weight_grad(ht, own, other, start, width_all, before=None):
    depth, rows = ht.shape
    width = own.shape[1]
    block = 512
    args = [ht, own, other]
    specs = [LOCAL] * 3
    aliases = {}
    if before is not None:
        args.append(before)
        specs.append(pl.BlockSpec(memory_space=pl.ANY))
        aliases = {3: 0}
    return _call(
        functools.partial(_weight_body, start, block),
        "weight_grad",
        args,
        [jax.ShapeDtypeStruct((depth, width_all), BF16)],
        _cost(2 * rows * depth * width, 2 * depth * width + 2 * rows * width),
        specs=specs,
        out_specs=[pl.BlockSpec(memory_space=pl.ANY)],
        scratch=[pltpu.VMEM((WRITES, depth, block), BF16), pltpu.SemaphoreType.DMA((WRITES,))],
        aliases=aliases,
    )[0]


def per_device(hidden, head_weight, teacher_ids, teacher_logprobs, valid, row_weight):
    count = lax.axis_size("vocab")
    bits = count.bit_length() - 1
    r = lax.axis_index("row")
    v = lax.axis_index("vocab")
    width = head_weight.shape[1]
    half, own_terms = teacher_ids.shape
    terms = own_terms * count
    swap = [(0, 1), (1, 0)]
    chunks = _split(width, 4)
    groups = [[0, 1], [2, 3]]
    weights = _local(head_weight)

    h = hidden[None]
    packed = jnp.stack([teacher_ids.T.astype(F32), teacher_logprobs.T])
    for b in reversed(range(bits)):
        far = lax.ppermute(h, "vocab", _xor(count, 1 << b))
        far_packed = lax.ppermute(packed, "vocab", _xor(count, 1 << b))
        far, far_packed = lax.optimization_barrier((far, far_packed))
        bit = (v >> b) & 1
        first = bit == r if b == bits - 1 else bit == 0
        h = jnp.stack([jnp.where(first, h, far), jnp.where(first, far, h)], axis=1)
        h = h.reshape((-1,) + hidden.shape)
        packed = jnp.concatenate([packed, far_packed], axis=1)
    h = h.reshape(-1, hidden.shape[1])
    packed = packed - jnp.array([1.0, 0.0], F32)[:, None, None] * (v * width).astype(F32)
    h, packed = lax.optimization_barrier((h, packed))
    ht = h.T

    parts = []
    for chunk in chunks:
        own, send = _partial_logits(h, weights, chunk)
        parts.append((own, lax.ppermute(send, "row", swap)))
    es, stats = [], []
    picks = rows = None
    for i, (own, recv) in enumerate(parts):
        e, picks, stat, *rest = _exponentials(
            own, recv, chunks, i, terms, packed=packed, rows=rows, picks=picks, before=stats
        )
        if i == 0:
            rows = rest
        es.append(e)
        stats.append(stat)
    joined = rest[0][:4]
    ids, lps = rows

    for b in range(bits):
        joined = _join_stats(joined, lax.ppermute(joined, "vocab", _xor(count, 1 << b)))
    scale = row_weight * valid.astype(F32)
    tot = jnp.concatenate([joined, scale[None], jnp.zeros((3, half), F32)], axis=0)

    grads = []
    for group in groups:
        own = _logit_grad(
            [es[q] for q in group], [stats[q] for q in group], picks, ids, lps, tot, [chunks[q] for q in group], terms
        )
        grads.append((own, lax.ppermute(own, "row", swap)))

    order = (jnp.arange(count, dtype=jnp.int32) ^ v) ^ (r * (count // 2))
    starts = [chunks[group[0]][0] for group in groups]
    (before,) = _feature_terms(*grads[0], weights, starts[0])
    keep, send = _feature_terms(*grads[1], weights, starts[1], before, order)

    keep = keep + lax.ppermute(send, "vocab", _xor(count, 1)).astype(F32)
    keep = keep.reshape((count // 2,) + hidden.shape)
    total = keep[0]
    for d in range(1, count // 2):
        far = lax.ppermute(keep[d].astype(BF16), "vocab", _xor(count, 2 * d))
        total = total + far.astype(F32)
    hidden_grad = total.astype(BF16)

    weight_grad = _weight_grad(ht, *grads[0], starts[0], width)
    weight_grad = _weight_grad(ht, *grads[1], starts[1], width, weight_grad)
    return hidden_grad, weight_grad


def solution(mesh):
    return jax.shard_map(
        per_device,
        mesh=mesh,
        in_specs=(
            P(("grp", "vocab"), "row"),
            P("row", "vocab"),
            P(("grp", "row"), "vocab"),
            P(("grp", "row"), "vocab"),
            P(("grp", "row")),
            P(("grp", "row")),
        ),
        out_specs=(P(("grp", "vocab"), "row"), P(("grp", "row"), "vocab")),
        check_vma=False,
    )
```

```python
import functools

import jax
import jax.numpy as jnp
from jax import lax
from jax.experimental import pallas as pl
from jax.experimental.pallas import tpu as pltpu
from jax.sharding import PartitionSpec as P

VMEM_LIMIT = 14 * 1024 * 1024
TILE = 8
STEP = 16
NT = (((1,), (1,)), ((), ()))
F32 = jnp.float32
BF16 = jnp.bfloat16
LOCAL = pl.BlockSpec(memory_space=pltpu.VMEM)
WRITES = 4


def _local(x):
    return pltpu.with_memory_space_constraint(x, pltpu.VMEM)


def _cost(flops, nbytes):
    return pl.CostEstimate(flops=int(flops), bytes_accessed=int(nbytes), transcendentals=0)


def _call(body, name, args, out_shape, cost, specs=None, out_specs=None, scratch=(), aliases=None):
    specs = specs or [LOCAL] * len(args)
    args = [_local(x) if s is LOCAL else x for x, s in zip(args, specs)]
    return pl.pallas_call(
        body,
        in_specs=specs,
        out_specs=out_specs or [LOCAL] * len(out_shape),
        out_shape=out_shape,
        scratch_shapes=list(scratch),
        input_output_aliases=aliases or {},
        compiler_params=pltpu.CompilerParams(vmem_limit_bytes=VMEM_LIMIT),
        cost_estimate=cost,
        name=name,
    )(*args)


def _split(width, count):
    unit = 256 if width % 256 == 0 else 128
    units = width // unit
    ends = [units * (i + 1) // count for i in range(count)]
    starts = [0] + ends[:-1]
    return [(a * unit, (b - a) * unit) for a, b in zip(starts, ends)]


def _blocks(width, block):
    return [(a, min(block, width - a)) for a in range(0, width, block)]


def _xor(n, s):
    return [(i, i ^ s) for i in range(n)]


def _logits_body(start, h_ref, w_ref, own_ref, send_ref):
    half = own_ref.shape[0]
    for at, size in _blocks(own_ref.shape[1], 1280):
        part = jnp.dot(h_ref[...], w_ref[:, start + at : start + at + size], preferred_element_type=F32)
        own_ref[:, at : at + size] = part[:half]
        send_ref[:, at : at + size] = part[half:]


def _partial_logits(h, w, chunk):
    start, width = chunk
    rows, depth = h.shape
    out = pltpu.VMEM((rows // 2, width), F32)
    return _call(
        functools.partial(_logits_body, start),
        "partial_logits",
        [h, w],
        [out, out],
        _cost(2 * rows * depth * width, 2 * depth * width + 4 * rows * width),
    )


def _exp_body(start, width, index, count, terms, kept, *refs):
    first, last = index == 0, index == count - 1
    refs = list(refs)
    own_ref, recv_ref = refs.pop(0), refs.pop(0)
    if first:
        packed_ref = refs.pop(0)
    else:
        ids_ref, lps_ref, picks_in = refs.pop(0), refs.pop(0), refs.pop(0)
    before = [refs.pop(0) for _ in range(index)] if last else []
    del refs[:kept]
    e_ref, picks_ref, stat_ref = refs.pop(0), refs.pop(0), refs.pop(0)
    half = own_ref.shape[0]
    if first:
        ids_ref, lps_ref = refs.pop(0), refs.pop(0)
        pad = jnp.full((128 - terms, half), -1.0, F32)
        ids_ref[...] = jnp.concatenate([packed_ref[0], pad], axis=0).T.astype(jnp.int32)
        lps_ref[...] = jnp.concatenate([packed_ref[1], pad], axis=0).T
    if last:
        tot_ref = refs.pop(0)
    hold = refs.pop(0)
    lane = lax.broadcasted_iota(jnp.int32, (half, 128), 1)
    ways = 4

    def pick(t, carry):
        rows = pl.ds(pl.multiple_of(t * TILE, TILE), TILE)
        rel = ids_ref[rows, :] - start
        key = rel >> 7
        slot = rel & 127
        acc = [jnp.zeros((TILE, 128), F32)] * ways
        top = [jnp.full((TILE, 128), -jnp.inf, F32)] * ways
        for c in range(width // 128):
            cols = slice(c * 128, (c + 1) * 128)
            w = c % ways
            logit = own_ref[rows, cols] + recv_ref[rows, cols]
            e_ref[rows, cols] = logit
            top[w] = jnp.maximum(top[w], logit)
            got = jnp.take_along_axis(logit, slot, axis=1, mode="promise_in_bounds")
            acc[w] = jnp.where(key == c, got, acc[w])
        hold[rows, :] = functools.reduce(jnp.maximum, top)
        picked = sum(acc)
        picks_ref[rows, :] = picked if first else picked + picks_in[rows, :]
        return carry

    def power(t, carry):
        rows = pl.ds(pl.multiple_of(t * TILE, TILE), TILE)
        top = stat_ref[rows, :]
        total = [jnp.zeros((TILE, 128), F32)] * ways
        for c in range(width // 128):
            cols = slice(c * 128, (c + 1) * 128)
            e = jnp.exp(e_ref[rows, cols] - top)
            e_ref[rows, cols] = e
            total[c % ways] += e
        hold[rows, :] = sum(total)
        return carry

    lax.fori_loop(0, half // TILE, pick, 0, unroll=2)
    stat_ref[...] = jnp.broadcast_to(jnp.max(hold[...], axis=1, keepdims=True), (half, 128))
    lax.fori_loop(0, half // TILE, power, 0, unroll=2)
    top = stat_ref[...]
    total = jnp.sum(hold[...], axis=1, keepdims=True)
    stat_ref[...] = jnp.where(lane == 0, top, total)
    if last:
        tops, totals = [top[:, 0:1]], [total]
        for ref in before:
            tops.append(ref[:, 0:1])
            totals.append(ref[:, 1:2])
        both = functools.reduce(jnp.maximum, tops)
        total = sum(s * jnp.exp(m - both) for m, s in zip(tops, totals))
        ids = ids_ref[...]
        inside = (ids >= 0) & (ids < start + width)
        picked = picks_ref[...] - both
        weight = jnp.where(inside, jnp.exp(picked), 0.0)
        mixed = jnp.sum(weight * (picked - lps_ref[...] + 1.0), axis=1, keepdims=True)
        plain = jnp.sum(weight, axis=1, keepdims=True)
        table = jnp.where(lane == 0, both, jnp.where(lane == 1, total, jnp.where(lane == 2, mixed, plain)))
        tot_ref[...] = table.T[:TILE, :]


def _exponentials(own, recv, chunks, index, terms, packed=None, rows=None, picks=None, before=(), kept=()):
    start, width = chunks[index]
    half = own.shape[0]
    first, last = index == 0, index == len(chunks) - 1
    table = pltpu.VMEM((half, 128), F32)
    args = [own, recv] + ([packed] if first else [*rows, picks]) + (list(before) if last else []) + list(kept)
    out = [pltpu.VMEM((half, width), F32), table, table]
    if first:
        out += [pltpu.VMEM((half, 128), jnp.int32), table]
    if last:
        out.append(pltpu.VMEM((TILE, half), F32))
    return _call(
        functools.partial(_exp_body, start, width, index, len(chunks), terms, len(kept)),
        "exponentials",
        args,
        out,
        _cost(8 * half * width, 12 * half * width),
        scratch=[pltpu.VMEM((half, 128), F32)],
    )


def _join_body(a_ref, b_ref, *refs):
    a, b = a_ref[...], b_ref[...]
    top = jnp.maximum(a[0:1], b[0:1])
    da, db = a[0:1] - top, b[0:1] - top
    fa, fb = jnp.exp(da), jnp.exp(db)
    total = a[1:2] * fa + b[1:2] * fb
    mixed = (a[2:3] + da * a[3:4]) * fa + (b[2:3] + db * b[3:4]) * fb
    plain = a[3:4] * fa + b[3:4] * fb
    refs[-1][...] = jnp.concatenate([top, total, mixed, plain, a[4:]], axis=0)


def _join_stats(a, b, kept):
    return _call(
        _join_body, "join_stats", [a, b, *kept], [pltpu.VMEM(a.shape, F32)], _cost(10 * a.size, 12 * a.size)
    )[0]


def _fetch_body(start, w_ref, out_ref, sems):
    depth = w_ref.shape[0]
    step = depth // sems.shape[0]
    copies = [
        pltpu.make_async_copy(
            w_ref.at[pl.ds(i * step, step), pl.ds(start, out_ref.shape[1])],
            out_ref.at[pl.ds(i * step, step), :],
            sems.at[i],
        )
        for i in range(sems.shape[0])
    ]
    for copy in copies:
        copy.start()
    for copy in copies:
        copy.wait()


def _fetch(w, start, width):
    depth = w.shape[0]
    return _call(
        functools.partial(_fetch_body, start),
        "fetch_weight",
        [pltpu.with_memory_space_constraint(w, pltpu.HBM)],
        [pltpu.VMEM((depth, width), BF16)],
        _cost(0, 2 * depth * width),
        specs=[pl.BlockSpec(memory_space=pltpu.HBM)],
        scratch=[pltpu.SemaphoreType.DMA((4,))],
    )[0]


def _grad_body(chunks, terms, *refs):
    count = len(chunks)
    e_refs, stat_refs = refs[:count], refs[count : 2 * count]
    picks_ref, ids_ref, lps_ref, tot_ref = refs[2 * count : 2 * count + 4]
    g_ref, coef_ref, high_ref, low_ref = refs[-4:]
    half = tot_ref.shape[1]
    lanes = TILE * terms
    begin = chunks[0][0]
    width = sum(w for _, w in chunks)
    parts = (width + 255) // 256

    tot = jnp.concatenate([tot_ref[...], jnp.zeros((128 - TILE, half), F32)], axis=0).T
    top, total, mixed, plain, scale = (tot[:, i : i + 1] for i in range(5))
    log_sum = jnp.log(total)
    lse = top + log_sum
    sum_grad = scale * jnp.exp(-log_sum) * (mixed - log_sum * plain)
    for q, ref in enumerate(stat_refs):
        coef_ref[q] = jnp.broadcast_to(sum_grad * jnp.exp(ref[:, 0:1] - lse), (half, 128))
    rel = ids_ref[...] - begin
    inside = (rel >= 0) & (rel < width)
    support = picks_ref[...] - lse
    grad = scale * jnp.exp(support) * (support - lps_ref[...] + 1.0)
    grad = jnp.where(inside, grad, 0.0)
    high = grad.astype(BF16).astype(F32)
    high_ref[...] = high
    low_ref[...] = grad - high

    lane_row = lax.broadcasted_iota(jnp.int32, (TILE, lanes), 1) // terms
    mask = lane_row == lax.broadcasted_iota(jnp.int32, (TILE, lanes), 0)
    place = lax.broadcasted_iota(jnp.int32, (256, lanes), 0)

    def flat(x):
        return jnp.concatenate([x[:, :terms]] * TILE, axis=1)

    def tile(t):
        rows = pl.ds(pl.multiple_of(t * TILE, TILE), TILE)
        rel = flat(ids_ref[rows, :]) - begin
        key = jnp.where(mask, rel >> 8, -1)
        col = jnp.sum(jnp.where(mask, rel & 255, 0), axis=0, keepdims=True)
        high, low = flat(high_ref[rows, :]), flat(low_ref[rows, :])
        lhs = jnp.concatenate(
            [
                jnp.concatenate([jnp.where(key == c, high, 0.0), jnp.where(key == c, low, 0.0)], axis=1)
                for c in range(parts)
            ],
            axis=0,
        ).astype(BF16)
        hot = (place == jnp.broadcast_to(col, (256, lanes))).astype(F32).astype(BF16)
        rhs = jnp.concatenate([hot, hot], axis=1)
        return rows, lax.dot_general(lhs, rhs, NT, preferred_element_type=F32)

    def step(i, carry):
        pair = [tile(i * (STEP // TILE) + t) for t in range(STEP // TILE)]
        out_rows = pl.ds(pl.multiple_of(i * STEP, STEP), STEP)
        for q, (start, w) in enumerate(chunks):
            coefs = [coef_ref[q, rows, :] for rows, _ in pair]
            for at, size in _blocks(w, 128):
                col = start - begin + at
                c, off = col // 256, col % 256
                out = [
                    s[c * TILE : (c + 1) * TILE, off : off + size] - e_refs[q][rows, at : at + size] * coef
                    for (rows, s), coef in zip(pair, coefs)
                ]
                g_ref[out_rows, col : col + size] = jnp.concatenate(out, axis=0).astype(BF16)
        return carry

    lax.fori_loop(0, half // STEP, step, 0, unroll=2)


def _logit_grad(es, stats, picks, ids, lps, tot, chunks, terms, kept):
    half = es[0].shape[0]
    width = sum(w for _, w in chunks)
    table = pltpu.VMEM((half, 128), F32)
    return _call(
        functools.partial(_grad_body, chunks, terms),
        "logit_grad",
        [*es, *stats, picks, ids, lps, tot, *kept],
        [pltpu.VMEM((half, width), BF16)],
        _cost(8 * half * width, 6 * half * width),
        scratch=[pltpu.VMEM((len(chunks), half, 128), F32), table, table],
    )[0]


def _feature_body(count, *refs):
    if count:
        own_ref, other_ref, w_ref, before_ref, order_ref, keep_ref, send_ref, acc = refs
    else:
        own_ref, other_ref, w_ref, acc = refs
    grads = jnp.concatenate([own_ref[...], other_ref[...]], axis=0)
    part = lax.dot_general(grads, w_ref[...], NT, preferred_element_type=F32)
    if not count:
        acc[...] = part
        return
    acc[...] = part + before_ref[...]
    rows = acc.shape[0] // count
    near, far = [], []
    for d in range(count):
        at = pl.multiple_of(order_ref[d] * rows, rows)
        (far if d % 2 else near).append(acc[pl.ds(at, rows), :])
    keep_ref[...] = jnp.concatenate(near, axis=0)
    send_ref[...] = jnp.concatenate(far, axis=0).astype(BF16)


def _feature_terms(own, other, w, before=None, order=None):
    half, width = own.shape
    depth = w.shape[0]
    args = [own, other, w]
    specs = [LOCAL] * 3
    scratch = []
    out = [pltpu.VMEM((2 * half, depth), F32)]
    if before is not None:
        args += [before, order]
        specs += [LOCAL, pl.BlockSpec(memory_space=pltpu.SMEM)]
        scratch = out
        out = [pltpu.VMEM((half, depth), F32), pltpu.VMEM((half, depth), BF16)]
    return _call(
        functools.partial(_feature_body, 0 if before is None else order.shape[0]),
        "feature_terms",
        args,
        out,
        _cost(4 * half * depth * width, 2 * depth * width + 4 * half * width),
        specs=specs,
        scratch=scratch,
    )


def _weight_body(start, block, ht_ref, own_ref, other_ref, *refs):
    out_ref, ring, sems = refs[-3:]
    copies = []
    for i, (at, size) in enumerate(_blocks(own_ref.shape[1], block)):
        slot = i % WRITES
        if i >= WRITES:
            copies[i - WRITES].wait()
        cols = slice(at, at + size)
        grads = jnp.concatenate([own_ref[:, cols], other_ref[:, cols]], axis=0)
        ring[slot, :, :size] = jnp.dot(ht_ref[...], grads, preferred_element_type=F32).astype(BF16)
        copy = pltpu.make_async_copy(
            ring.at[slot, :, pl.ds(0, size)], out_ref.at[:, pl.ds(start + at, size)], sems.at[slot]
        )
        copy.start()
        copies.append(copy)
    for copy in copies[-WRITES:]:
        copy.wait()


def _weight_grad(ht, own, other, start, width_all, before=None):
    depth, rows = ht.shape
    width = own.shape[1]
    block = 512
    args = [ht, own, other]
    specs = [LOCAL] * 3
    aliases = {}
    if before is not None:
        args.append(before)
        specs.append(pl.BlockSpec(memory_space=pl.ANY))
        aliases = {3: 0}
    return _call(
        functools.partial(_weight_body, start, block),
        "weight_grad",
        args,
        [jax.ShapeDtypeStruct((depth, width_all), BF16)],
        _cost(2 * rows * depth * width, 2 * depth * width + 2 * rows * width),
        specs=specs,
        out_specs=[pl.BlockSpec(memory_space=pl.ANY)],
        scratch=[pltpu.VMEM((WRITES, depth, block), BF16), pltpu.SemaphoreType.DMA((WRITES,))],
        aliases=aliases,
    )[0]


def per_device(hidden, head_weight, teacher_ids, teacher_logprobs, valid, row_weight):
    count = lax.axis_size("vocab")
    bits = count.bit_length() - 1
    r = lax.axis_index("row")
    v = lax.axis_index("vocab")
    width = head_weight.shape[1]
    half, own_terms = teacher_ids.shape
    terms = own_terms * count
    swap = [(0, 1), (1, 0)]
    chunks = _split(width, 4)
    groups = [[0, 1], [2, 3]]
    starts = [chunks[group[0]][0] for group in groups]
    widths = [sum(chunks[q][1] for q in group) for group in groups]

    h = hidden[None]
    packed = jnp.stack([teacher_ids.T.astype(F32), teacher_logprobs.T])
    weights = []
    for b in reversed(range(bits)):
        far = lax.ppermute(h, "vocab", _xor(count, 1 << b))
        far_packed = lax.ppermute(packed, "vocab", _xor(count, 1 << b))
        if b < 2:
            g = len(weights)
            _, source = lax.optimization_barrier((h, head_weight))
            part = _fetch(source, starts[g], widths[g])
            far, far_packed, part = lax.optimization_barrier((far, far_packed, part))
            weights.append(part)
        else:
            far, far_packed = lax.optimization_barrier((far, far_packed))
        bit = (v >> b) & 1
        first = bit == r if b == bits - 1 else bit == 0
        h = jnp.stack([jnp.where(first, h, far), jnp.where(first, far, h)], axis=1)
        h = h.reshape((-1,) + hidden.shape)
        packed = jnp.concatenate([packed, far_packed], axis=1)
    h = h.reshape(-1, hidden.shape[1])
    packed = packed - jnp.array([1.0, 0.0], F32)[:, None, None] * (v * width).astype(F32)
    h, packed = lax.optimization_barrier((h, packed))
    ht = h.T

    parts = []
    for i, (start, size) in enumerate(chunks):
        g = 0 if i in groups[0] else 1
        own, send = _partial_logits(h, weights[g], (start - starts[g], size))
        parts.append((own, lax.ppermute(send, "row", swap)))
    es, stats = [], []
    picks = rows = None
    for i, (own, recv) in enumerate(parts):
        e, picks, stat, *rest = _exponentials(
            own, recv, chunks, i, terms, packed=packed, rows=rows, picks=picks, before=stats, kept=[*weights, *es]
        )
        if i == 0:
            rows = rest
        es.append(e)
        stats.append(stat)
    ids, lps = rows

    scale = row_weight * valid.astype(F32)
    joined = jnp.concatenate([rest[0][:4], scale[None], jnp.zeros((3, half), F32)], axis=0)
    for b in range(bits):
        far = lax.ppermute(joined, "vocab", _xor(count, 1 << b))
        joined = _join_stats(joined, far, [*weights, *es, *stats, picks, ids, lps])

    grads = []
    for group in groups:
        own = _logit_grad(
            [es[q] for q in group],
            [stats[q] for q in group],
            picks,
            ids,
            lps,
            joined,
            [chunks[q] for q in group],
            terms,
            weights,
        )
        grads.append((own, lax.ppermute(own, "row", swap)))

    order = (jnp.arange(count, dtype=jnp.int32) ^ v) ^ (r * (count // 2))
    (before,) = _feature_terms(*grads[0], weights[0])
    keep, send = _feature_terms(*grads[1], weights[1], before, order)

    keep = keep + lax.ppermute(send, "vocab", _xor(count, 1)).astype(F32)
    keep = keep.reshape((count // 2,) + hidden.shape)
    total = keep[0]
    for d in range(1, count // 2):
        far = lax.ppermute(keep[d].astype(BF16), "vocab", _xor(count, 2 * d))
        total = total + far.astype(F32)
    hidden_grad = total.astype(BF16)

    weight_grad = _weight_grad(ht, *grads[0], starts[0], width)
    weight_grad = _weight_grad(ht, *grads[1], starts[1], width, weight_grad)
    return hidden_grad, weight_grad


def solution(mesh):
    return jax.shard_map(
        per_device,
        mesh=mesh,
        in_specs=(
            P(("grp", "vocab"), "row"),
            P("row", "vocab"),
            P(("grp", "row"), "vocab"),
            P(("grp", "row"), "vocab"),
            P(("grp", "row")),
            P(("grp", "row")),
        ),
        out_specs=(P(("grp", "vocab"), "row"), P(("grp", "row"), "vocab")),
        check_vma=False,
    )
```

```python
import functools

import jax
import jax.numpy as jnp
from jax import lax
from jax.experimental import pallas as pl
from jax.experimental.pallas import tpu as pltpu
from jax.sharding import PartitionSpec as P

MIB = 1024 * 1024
TILE = 8
STEP = 16
NT = (((1,), (1,)), ((), ()))
F32 = jnp.float32
BF16 = jnp.bfloat16
LOCAL = pl.BlockSpec(memory_space=pltpu.VMEM)
REMOTE = pl.BlockSpec(memory_space=pltpu.HBM)
WRITES = 4


def _local(x):
    return pltpu.with_memory_space_constraint(x, pltpu.VMEM)


def _cost(flops, nbytes):
    return pl.CostEstimate(flops=int(flops), bytes_accessed=int(nbytes), transcendentals=0)


def _call(body, name, args, out_shape, cost, specs=None, out_specs=None, scratch=(), aliases=None, limit=8):
    specs = specs or [LOCAL] * len(args)
    args = [
        _local(x) if s is LOCAL else pltpu.with_memory_space_constraint(x, pltpu.HBM) if s is REMOTE else x
        for x, s in zip(args, specs)
    ]
    return pl.pallas_call(
        body,
        in_specs=specs,
        out_specs=out_specs or [LOCAL] * len(out_shape),
        out_shape=out_shape,
        scratch_shapes=list(scratch),
        input_output_aliases=aliases or {},
        compiler_params=pltpu.CompilerParams(vmem_limit_bytes=limit * MIB),
        cost_estimate=cost,
        name=name,
    )(*args)


def _split(width, count):
    unit = 256 if width % 256 == 0 else 128
    units = width // unit
    ends = [units * (i + 1) // count for i in range(count)]
    starts = [0] + ends[:-1]
    return [(a * unit, (b - a) * unit) for a, b in zip(starts, ends)]


def _blocks(width, block):
    return [(a, min(block, width - a)) for a in range(0, width, block)]


def _xor(n, s):
    return [(i, i ^ s) for i in range(n)]


def _copies(w_ref, start, out_ref, sems):
    depth, width = out_ref.shape
    step = depth // sems.shape[0]
    return [
        pltpu.make_async_copy(
            w_ref.at[pl.ds(i * step, step), pl.ds(start, width)], out_ref.at[pl.ds(i * step, step), :], sems.at[i]
        )
        for i in range(sems.shape[0])
    ]


def _fetch_body(start, w_ref, out_ref, sems):
    copies = _copies(w_ref, start, out_ref, sems)
    for copy in copies:
        copy.start()
    for copy in copies:
        copy.wait()


def _fetch(w, start, width):
    depth = w.shape[0]
    return _call(
        functools.partial(_fetch_body, start),
        "fetch_weight",
        [w],
        [pltpu.VMEM((depth, width), BF16)],
        _cost(0, 2 * depth * width),
        specs=[REMOTE],
        scratch=[pltpu.SemaphoreType.DMA((4,))],
    )[0]


def _logits_body(start, after, h_ref, w_ref, *refs):
    if after is not None:
        source_ref, own_ref, send_ref, next_ref, sems = refs
        copies = _copies(source_ref, after, next_ref, sems)
        for copy in copies:
            copy.start()
    else:
        own_ref, send_ref = refs
    half = own_ref.shape[0]
    for at, size in _blocks(own_ref.shape[1], 1280):
        part = jnp.dot(h_ref[...], w_ref[:, start + at : start + at + size], preferred_element_type=F32)
        own_ref[:, at : at + size] = part[:half]
        send_ref[:, at : at + size] = part[half:]
    if after is not None:
        for copy in copies:
            copy.wait()


def _partial_logits(h, w, chunk, source=None, after=None):
    start, width = chunk
    rows, depth = h.shape
    out = pltpu.VMEM((rows // 2, width), F32)
    args, specs, outs, scratch = [h, w], [LOCAL, LOCAL], [out, out], []
    if after is not None:
        args.append(source)
        specs.append(REMOTE)
        outs.append(pltpu.VMEM((depth, after[1]), BF16))
        scratch = [pltpu.SemaphoreType.DMA((4,))]
    return _call(
        functools.partial(_logits_body, start, after and after[0]),
        "partial_logits",
        args,
        outs,
        _cost(2 * rows * depth * width, 2 * depth * width + 4 * rows * width),
        specs=specs,
        scratch=scratch,
    )


def _exp_body(start, width, index, count, terms, kept, *refs):
    first, last = index == 0, index == count - 1
    refs = list(refs)
    own_ref, recv_ref = refs.pop(0), refs.pop(0)
    if first:
        packed_ref = refs.pop(0)
    else:
        ids_ref, lps_ref, picks_in = refs.pop(0), refs.pop(0), refs.pop(0)
    before = [refs.pop(0) for _ in range(index)] if last else []
    del refs[:kept]
    e_ref, picks_ref, stat_ref = refs.pop(0), refs.pop(0), refs.pop(0)
    half = own_ref.shape[0]
    if first:
        ids_ref, lps_ref = refs.pop(0), refs.pop(0)
        pad = jnp.full((128 - terms, half), -1.0, F32)
        ids_ref[...] = jnp.concatenate([packed_ref[0], pad], axis=0).T.astype(jnp.int32)
        lps_ref[...] = jnp.concatenate([packed_ref[1], pad], axis=0).T
    if last:
        tot_ref = refs.pop(0)
    hold = refs.pop(0)
    lane = lax.broadcasted_iota(jnp.int32, (half, 128), 1)
    ways = 4

    def pick(t, carry):
        rows = pl.ds(pl.multiple_of(t * TILE, TILE), TILE)
        rel = ids_ref[rows, :] - start
        key = rel >> 7
        slot = rel & 127
        acc = [jnp.zeros((TILE, 128), F32)] * ways
        top = [jnp.full((TILE, 128), -jnp.inf, F32)] * ways
        for c in range(width // 128):
            cols = slice(c * 128, (c + 1) * 128)
            w = c % ways
            logit = own_ref[rows, cols] + recv_ref[rows, cols]
            e_ref[rows, cols] = logit
            top[w] = jnp.maximum(top[w], logit)
            got = jnp.take_along_axis(logit, slot, axis=1, mode="promise_in_bounds")
            acc[w] = jnp.where(key == c, got, acc[w])
        hold[rows, :] = functools.reduce(jnp.maximum, top)
        picked = sum(acc)
        picks_ref[rows, :] = picked if first else picked + picks_in[rows, :]
        return carry

    def power(t, carry):
        rows = pl.ds(pl.multiple_of(t * TILE, TILE), TILE)
        top = stat_ref[rows, :]
        total = [jnp.zeros((TILE, 128), F32)] * ways
        for c in range(width // 128):
            cols = slice(c * 128, (c + 1) * 128)
            e = jnp.exp(e_ref[rows, cols] - top)
            e_ref[rows, cols] = e
            total[c % ways] += e
        hold[rows, :] = sum(total)
        return carry

    lax.fori_loop(0, half // TILE, pick, 0, unroll=2)
    stat_ref[...] = jnp.broadcast_to(jnp.max(hold[...], axis=1, keepdims=True), (half, 128))
    lax.fori_loop(0, half // TILE, power, 0, unroll=2)
    top = stat_ref[...]
    total = jnp.sum(hold[...], axis=1, keepdims=True)
    stat_ref[...] = jnp.where(lane == 0, top, total)
    if last:
        tops, totals = [top[:, 0:1]], [total]
        for ref in before:
            tops.append(ref[:, 0:1])
            totals.append(ref[:, 1:2])
        both = functools.reduce(jnp.maximum, tops)
        total = sum(s * jnp.exp(m - both) for m, s in zip(tops, totals))
        ids = ids_ref[...]
        inside = (ids >= 0) & (ids < start + width)
        picked = picks_ref[...] - both
        weight = jnp.where(inside, jnp.exp(picked), 0.0)
        mixed = jnp.sum(weight * (picked - lps_ref[...] + 1.0), axis=1, keepdims=True)
        plain = jnp.sum(weight, axis=1, keepdims=True)
        table = jnp.where(lane == 0, both, jnp.where(lane == 1, total, jnp.where(lane == 2, mixed, plain)))
        tot_ref[...] = table.T[:TILE, :]


def _exponentials(own, recv, chunks, index, terms, packed=None, rows=None, picks=None, before=(), kept=()):
    start, width = chunks[index]
    half = own.shape[0]
    first, last = index == 0, index == len(chunks) - 1
    table = pltpu.VMEM((half, 128), F32)
    args = [own, recv] + ([packed] if first else [*rows, picks]) + (list(before) if last else []) + list(kept)
    out = [pltpu.VMEM((half, width), F32), table, table]
    if first:
        out += [pltpu.VMEM((half, 128), jnp.int32), table]
    if last:
        out.append(pltpu.VMEM((TILE, half), F32))
    return _call(
        functools.partial(_exp_body, start, width, index, len(chunks), terms, len(kept)),
        "exponentials",
        args,
        out,
        _cost(8 * half * width, 12 * half * width),
        scratch=[pltpu.VMEM((half, 128), F32)],
    )


def _join_body(a_ref, b_ref, *refs):
    a, b = a_ref[...], b_ref[...]
    top = jnp.maximum(a[0:1], b[0:1])
    da, db = a[0:1] - top, b[0:1] - top
    fa, fb = jnp.exp(da), jnp.exp(db)
    total = a[1:2] * fa + b[1:2] * fb
    mixed = (a[2:3] + da * a[3:4]) * fa + (b[2:3] + db * b[3:4]) * fb
    plain = a[3:4] * fa + b[3:4] * fb
    refs[-1][...] = jnp.concatenate([top, total, mixed, plain, a[4:]], axis=0)


def _join_stats(a, b, kept):
    return _call(
        _join_body, "join_stats", [a, b, *kept], [pltpu.VMEM(a.shape, F32)], _cost(10 * a.size, 12 * a.size)
    )[0]


def _grad_body(chunks, terms, *refs):
    count = len(chunks)
    e_refs, stat_refs = refs[:count], refs[count : 2 * count]
    picks_ref, ids_ref, lps_ref, tot_ref = refs[2 * count : 2 * count + 4]
    g_ref, coef_ref, high_ref, low_ref = refs[-4:]
    half = tot_ref.shape[1]
    lanes = TILE * terms
    begin = chunks[0][0]
    width = sum(w for _, w in chunks)
    parts = (width + 255) // 256

    tot = jnp.concatenate([tot_ref[...], jnp.zeros((128 - TILE, half), F32)], axis=0).T
    top, total, mixed, plain, scale = (tot[:, i : i + 1] for i in range(5))
    log_sum = jnp.log(total)
    lse = top + log_sum
    sum_grad = scale * jnp.exp(-log_sum) * (mixed - log_sum * plain)
    for q, ref in enumerate(stat_refs):
        coef_ref[q] = jnp.broadcast_to(sum_grad * jnp.exp(ref[:, 0:1] - lse), (half, 128))
    rel = ids_ref[...] - begin
    inside = (rel >= 0) & (rel < width)
    support = picks_ref[...] - lse
    grad = scale * jnp.exp(support) * (support - lps_ref[...] + 1.0)
    grad = jnp.where(inside, grad, 0.0)
    high = grad.astype(BF16).astype(F32)
    high_ref[...] = high
    low_ref[...] = grad - high

    lane_row = lax.broadcasted_iota(jnp.int32, (TILE, lanes), 1) // terms
    mask = lane_row == lax.broadcasted_iota(jnp.int32, (TILE, lanes), 0)
    place = lax.broadcasted_iota(jnp.int32, (256, lanes), 0)

    def flat(x):
        return jnp.concatenate([x[:, :terms]] * TILE, axis=1)

    def tile(t):
        rows = pl.ds(pl.multiple_of(t * TILE, TILE), TILE)
        rel = flat(ids_ref[rows, :]) - begin
        key = jnp.where(mask, rel >> 8, -1)
        col = jnp.sum(jnp.where(mask, rel & 255, 0), axis=0, keepdims=True)
        high, low = flat(high_ref[rows, :]), flat(low_ref[rows, :])
        lhs = jnp.concatenate(
            [
                jnp.concatenate([jnp.where(key == c, high, 0.0), jnp.where(key == c, low, 0.0)], axis=1)
                for c in range(parts)
            ],
            axis=0,
        ).astype(BF16)
        hot = (place == jnp.broadcast_to(col, (256, lanes))).astype(F32).astype(BF16)
        rhs = jnp.concatenate([hot, hot], axis=1)
        return rows, lax.dot_general(lhs, rhs, NT, preferred_element_type=F32)

    def step(i, carry):
        pair = [tile(i * (STEP // TILE) + t) for t in range(STEP // TILE)]
        out_rows = pl.ds(pl.multiple_of(i * STEP, STEP), STEP)
        for q, (start, w) in enumerate(chunks):
            coefs = [coef_ref[q, rows, :] for rows, _ in pair]
            for at, size in _blocks(w, 128):
                col = start - begin + at
                c, off = col // 256, col % 256
                out = [
                    s[c * TILE : (c + 1) * TILE, off : off + size] - e_refs[q][rows, at : at + size] * coef
                    for (rows, s), coef in zip(pair, coefs)
                ]
                g_ref[out_rows, col : col + size] = jnp.concatenate(out, axis=0).astype(BF16)
        return carry

    lax.fori_loop(0, half // STEP, step, 0, unroll=2)


def _logit_grad(es, stats, picks, ids, lps, tot, chunks, terms):
    half = es[0].shape[0]
    width = sum(w for _, w in chunks)
    table = pltpu.VMEM((half, 128), F32)
    return _call(
        functools.partial(_grad_body, chunks, terms),
        "logit_grad",
        [*es, *stats, picks, ids, lps, tot],
        [pltpu.VMEM((half, width), BF16)],
        _cost(8 * half * width, 6 * half * width),
        scratch=[pltpu.VMEM((len(chunks), half, 128), F32), table, table],
    )[0]


def _feature_body(start, block, count, *refs):
    if count:
        own_ref, far_ref, w_ref, before_ref, order_ref, keep_ref, send_ref, acc, other, weights, sems = refs
    else:
        own_ref, far_ref, w_ref, acc, other, weights, sems = refs
    blocks = _blocks(own_ref.shape[1], block)
    copies = [pltpu.make_async_copy(far_ref, other, sems.at[len(blocks)])] + [
        pltpu.make_async_copy(w_ref.at[:, pl.ds(start + at, size)], weights.at[:, pl.ds(at, size)], sems.at[i])
        for i, (at, size) in enumerate(blocks)
    ]
    for copy in copies:
        copy.start()
    copies[0].wait()
    for i, (at, size) in enumerate(blocks):
        cols = slice(at, at + size)
        grads = jnp.concatenate([own_ref[:, cols], other[:, cols]], axis=0)
        copies[i + 1].wait()
        part = lax.dot_general(grads, weights[:, cols], NT, preferred_element_type=F32)
        if i:
            acc[...] += part
        else:
            acc[...] = part + before_ref[...] if count else part
    if not count:
        return
    rows = acc.shape[0] // count
    near, far = [], []
    for d in range(count):
        at = pl.multiple_of(order_ref[d] * rows, rows)
        (far if d % 2 else near).append(acc[pl.ds(at, rows), :])
    keep_ref[...] = jnp.concatenate(near, axis=0)
    send_ref[...] = jnp.concatenate(far, axis=0).astype(BF16)


def _feature_terms(own, other, w, start, before=None, order=None):
    half, width = own.shape
    depth = w.shape[0]
    block = 1024
    args = [own, other, w]
    specs = [LOCAL, REMOTE, REMOTE]
    scratch = [
        pltpu.VMEM((half, width), BF16),
        pltpu.VMEM((depth, width), BF16),
        pltpu.SemaphoreType.DMA((len(_blocks(width, block)) + 1,)),
    ]
    out = [pltpu.VMEM((2 * half, depth), F32)]
    if before is not None:
        args += [before, order]
        specs += [LOCAL, pl.BlockSpec(memory_space=pltpu.SMEM)]
        scratch = out + scratch
        out = [pltpu.VMEM((half, depth), F32), pltpu.VMEM((half, depth), BF16)]
    return _call(
        functools.partial(_feature_body, start, block, 0 if before is None else order.shape[0]),
        "feature_terms",
        args,
        out,
        _cost(4 * half * depth * width, 2 * depth * width + 4 * half * width),
        specs=specs,
        scratch=scratch,
        limit=20,
    )


def _weight_body(start, block, ht_ref, own_ref, far_ref, *refs):
    out_ref, ring, other, sems = refs[-4:]
    fetch = pltpu.make_async_copy(far_ref, other, sems.at[WRITES])
    fetch.start()
    fetch.wait()
    copies = []
    for i, (at, size) in enumerate(_blocks(own_ref.shape[1], block)):
        slot = i % WRITES
        if i >= WRITES:
            copies[i - WRITES].wait()
        cols = slice(at, at + size)
        grads = jnp.concatenate([own_ref[:, cols], other[:, cols]], axis=0)
        ring[slot, :, :size] = jnp.dot(ht_ref[...], grads, preferred_element_type=F32).astype(BF16)
        copy = pltpu.make_async_copy(
            ring.at[slot, :, pl.ds(0, size)], out_ref.at[:, pl.ds(start + at, size)], sems.at[slot]
        )
        copy.start()
        copies.append(copy)
    for copy in copies[-WRITES:]:
        copy.wait()


def _weight_grad(ht, own, other, start, width_all, before=None, kept=()):
    depth, rows = ht.shape
    half, width = own.shape
    block = 1024
    args = [ht, own, other]
    specs = [LOCAL, LOCAL, REMOTE]
    aliases = {}
    if before is not None:
        args.append(before)
        specs.append(pl.BlockSpec(memory_space=pl.ANY))
        aliases = {3: 0}
    return _call(
        functools.partial(_weight_body, start, block),
        "weight_grad",
        [*args, *kept],
        [jax.ShapeDtypeStruct((depth, width_all), BF16)],
        _cost(2 * rows * depth * width, 2 * depth * width + 2 * rows * width),
        specs=specs + [LOCAL] * len(kept),
        out_specs=[pl.BlockSpec(memory_space=pl.ANY)],
        scratch=[
            pltpu.VMEM((WRITES, depth, block), BF16),
            pltpu.VMEM((half, width), BF16),
            pltpu.SemaphoreType.DMA((WRITES + 1,)),
        ],
        aliases=aliases,
        limit=16,
    )[0]


def per_device(hidden, head_weight, teacher_ids, teacher_logprobs, valid, row_weight):
    count = lax.axis_size("vocab")
    bits = count.bit_length() - 1
    r = lax.axis_index("row")
    v = lax.axis_index("vocab")
    width = head_weight.shape[1]
    half, own_terms = teacher_ids.shape
    terms = own_terms * count
    swap = [(0, 1), (1, 0)]
    chunks = _split(width, 4)
    groups = [[0, 1], [2, 3]]
    starts = [chunks[group[0]][0] for group in groups]
    widths = [sum(chunks[q][1] for q in group) for group in groups]

    h = hidden[None]
    packed = jnp.stack([teacher_ids.T.astype(F32), teacher_logprobs.T])
    for b in reversed(range(bits)):
        far = lax.ppermute(h, "vocab", _xor(count, 1 << b))
        far_packed = lax.ppermute(packed, "vocab", _xor(count, 1 << b))
        if b == 0:
            _, source = lax.optimization_barrier((h, head_weight))
            weights = _fetch(source, starts[0], widths[0])
            far, far_packed, weights = lax.optimization_barrier((far, far_packed, weights))
        else:
            far, far_packed = lax.optimization_barrier((far, far_packed))
        bit = (v >> b) & 1
        first = bit == r if b == bits - 1 else bit == 0
        h = jnp.stack([jnp.where(first, h, far), jnp.where(first, far, h)], axis=1)
        h = h.reshape((-1,) + hidden.shape)
        packed = jnp.concatenate([packed, far_packed], axis=1)
    h = h.reshape(-1, hidden.shape[1])
    packed = packed - jnp.array([1.0, 0.0], F32)[:, None, None] * (v * width).astype(F32)
    h, packed = lax.optimization_barrier((h, packed))
    ht = h.T

    parts, ready = [], {}
    for i, (start, size) in enumerate(chunks):
        if i in groups[0]:
            own, send, ready[i] = _partial_logits(
                h, weights, (start, size), head_weight, chunks[i + len(groups[0])]
            )
        else:
            own, send = _partial_logits(h, ready[i - len(groups[0])], (0, size))
        parts.append((own, lax.ppermute(send, "row", swap)))
    es, stats = [], []
    picks = rows = None
    for i, (own, recv) in enumerate(parts):
        e, picks, stat, *rest = _exponentials(
            own, recv, chunks, i, terms, packed=packed, rows=rows, picks=picks, before=stats, kept=es
        )
        if i == 0:
            rows = rest
        es.append(e)
        stats.append(stat)
    ids, lps = rows

    scale = row_weight * valid.astype(F32)
    joined = jnp.concatenate([rest[0][:4], scale[None], jnp.zeros((3, half), F32)], axis=0)
    for b in range(bits):
        far = lax.ppermute(joined, "vocab", _xor(count, 1 << b))
        joined = _join_stats(joined, far, [*es, *stats, picks, ids, lps])

    grads = []
    for group in groups:
        own = _logit_grad(
            [es[q] for q in group],
            [stats[q] for q in group],
            picks,
            ids,
            lps,
            joined,
            [chunks[q] for q in group],
            terms,
        )
        grads.append((own, lax.ppermute(own, "row", swap)))

    order = (jnp.arange(count, dtype=jnp.int32) ^ v) ^ (r * (count // 2))
    (before,) = _feature_terms(*grads[0], head_weight, starts[0])
    keep, send = _feature_terms(*grads[1], head_weight, starts[1], before, order)

    far = lax.ppermute(send, "vocab", _xor(count, 1))
    weight_grad = _weight_grad(ht, *grads[0], starts[0], width, kept=[keep])
    keep = keep + far.astype(F32)
    keep = keep.reshape((count // 2,) + hidden.shape)
    total = keep[0]
    for d in range(1, count // 2):
        far = lax.ppermute(keep[d].astype(BF16), "vocab", _xor(count, 2 * d))
        total = total + far.astype(F32)
    hidden_grad = total.astype(BF16)

    weight_grad = _weight_grad(ht, *grads[1], starts[1], width, weight_grad)
    return hidden_grad, weight_grad


def solution(mesh):
    return jax.shard_map(
        per_device,
        mesh=mesh,
        in_specs=(
            P(("grp", "vocab"), "row"),
            P("row", "vocab"),
            P(("grp", "row"), "vocab"),
            P(("grp", "row"), "vocab"),
            P(("grp", "row")),
            P(("grp", "row")),
        ),
        out_specs=(P(("grp", "vocab"), "row"), P(("grp", "row"), "vocab")),
        check_vma=False,
    )
```

```python
import functools

import jax
import jax.numpy as jnp
from jax import lax
from jax.experimental import pallas as pl
from jax.experimental.pallas import tpu as pltpu
from jax.sharding import PartitionSpec as P

MIB = 1024 * 1024
TILE = 8
STEP = 16
NT = (((1,), (1,)), ((), ()))
F32 = jnp.float32
BF16 = jnp.bfloat16
LOCAL = pl.BlockSpec(memory_space=pltpu.VMEM)
REMOTE = pl.BlockSpec(memory_space=pltpu.HBM)
WRITES = 4
GROUPS = 4
BLOCK = 1024
WIDE = 1280


def _local(x):
    return pltpu.with_memory_space_constraint(x, pltpu.VMEM)


def _cost(flops, nbytes):
    return pl.CostEstimate(flops=int(flops), bytes_accessed=int(nbytes), transcendentals=0)


def _copies(w_ref, start, out_ref, sems):
    depth, width = out_ref.shape
    step = depth // GROUPS
    return [
        pltpu.make_async_copy(
            w_ref.at[pl.ds(i * step, step), pl.ds(start, width)], out_ref.at[pl.ds(i * step, step), :], sems.at[i]
        )
        for i in range(GROUPS)
    ]


def _bringing(body, inputs, outputs, pieces):
    def wrapped(*refs):
        first = inputs + 1 + outputs
        news = refs[first : first + len(pieces)]
        sems = refs[-1]
        copies = []
        for i, ((start, _), ref) in enumerate(zip(pieces, news)):
            copies += _copies(refs[inputs], start, ref, sems.at[i])
        for copy in copies:
            copy.start()
        body(*refs[:inputs], *refs[inputs + 1 : first], *refs[first + len(pieces) : -1])
        for copy in copies:
            copy.wait()

    return wrapped


def _call(body, name, args, out_shape, cost, specs=None, out_specs=None, scratch=(), aliases=None, limit=8, bring=None):
    args, out_shape, scratch = list(args), list(out_shape), list(scratch)
    specs = list(specs or [LOCAL] * len(args))
    out_specs = list(out_specs or [LOCAL] * len(out_shape))
    if bring:
        source, pieces = bring
        body = _bringing(body, len(args), len(out_shape), pieces)
        args.append(source)
        specs.append(REMOTE)
        out_shape += [pltpu.VMEM((source.shape[0], width), source.dtype) for _, width in pieces]
        out_specs += [LOCAL] * len(pieces)
        scratch.append(pltpu.SemaphoreType.DMA((len(pieces), GROUPS)))
    args = [
        _local(x) if s is LOCAL else pltpu.with_memory_space_constraint(x, pltpu.HBM) if s is REMOTE else x
        for x, s in zip(args, specs)
    ]
    return pl.pallas_call(
        body,
        in_specs=specs,
        out_specs=out_specs,
        out_shape=out_shape,
        scratch_shapes=scratch,
        input_output_aliases=aliases or {},
        compiler_params=pltpu.CompilerParams(vmem_limit_bytes=limit * MIB),
        cost_estimate=cost,
        name=name,
    )(*args)


def _split(width, count):
    unit = 256 if width % 256 == 0 else 128
    units = width // unit
    ends = [units * (i + 1) // count for i in range(count)]
    starts = [0] + ends[:-1]
    return [(a * unit, (b - a) * unit) for a, b in zip(starts, ends)]


def _blocks(width, block):
    return [(a, min(block, width - a)) for a in range(0, width, block)]


def _xor(n, s):
    return [(i, i ^ s) for i in range(n)]


def _fetch(source, pieces):
    size = sum(width for _, width in pieces)
    return _call(lambda: None, "fetch_weight", [], [], _cost(0, 2 * source.shape[0] * size), bring=(source, pieces))


def _logits_body(count, turn, h_ref, *refs):
    w_refs = refs[:count]
    own_ref, send_ref = refs[count : count + 2]
    if turn:
        out_ref, turned, sem = refs[count + 2 :]
        turned[...] = h_ref[...].T
        copy = pltpu.make_async_copy(turned, out_ref, sem.at[0])
        copy.start()
    half = own_ref.shape[0]
    begin = 0
    for w_ref in w_refs:
        for at, size in _blocks(w_ref.shape[1], 1280):
            part = jnp.dot(h_ref[...], w_ref[:, at : at + size], preferred_element_type=F32)
            own_ref[:, begin + at : begin + at + size] = part[:half]
            send_ref[:, begin + at : begin + at + size] = part[half:]
        begin += w_ref.shape[1]
    if turn:
        copy.wait()


def _partial_logits(h, weights, turn=False, bring=None):
    rows, depth = h.shape
    width = sum(w.shape[1] for w in weights)
    out = [pltpu.VMEM((rows // 2, width), F32)] * 2
    out_specs, scratch = [LOCAL] * 2, []
    if turn:
        out.append(pltpu.HBM((depth, rows), BF16))
        out_specs.append(REMOTE)
        scratch = [pltpu.VMEM((depth, rows), BF16), pltpu.SemaphoreType.DMA((1,))]
    return _call(
        functools.partial(_logits_body, len(weights), turn),
        "partial_logits",
        [h, *weights],
        out,
        _cost(2 * rows * depth * width, 2 * depth * width + 4 * rows * width),
        out_specs=out_specs,
        scratch=scratch,
        bring=bring,
    )


def _exp_body(start, width, index, count, terms, kept, *refs):
    first, last = index == 0, index == count - 1
    refs = list(refs)
    own_ref, recv_ref = refs.pop(0), refs.pop(0)
    if first:
        packed_ref = refs.pop(0)
    else:
        ids_ref, lps_ref, picks_in = refs.pop(0), refs.pop(0), refs.pop(0)
    before = [refs.pop(0) for _ in range(index)] if last else []
    del refs[:kept]
    e_ref, picks_ref, stat_ref = refs.pop(0), refs.pop(0), refs.pop(0)
    half = own_ref.shape[0]
    if first:
        ids_ref, lps_ref = refs.pop(0), refs.pop(0)
        pad = jnp.full((128 - terms, half), -1.0, F32)
        ids_ref[...] = jnp.concatenate([packed_ref[0], pad], axis=0).T.astype(jnp.int32)
        lps_ref[...] = jnp.concatenate([packed_ref[1], pad], axis=0).T
    if last:
        tot_ref = refs.pop(0)
    hold = refs.pop(0)
    lane = lax.broadcasted_iota(jnp.int32, (half, 128), 1)
    ways = 4

    def pick(t, carry):
        rows = pl.ds(pl.multiple_of(t * TILE, TILE), TILE)
        rel = ids_ref[rows, :] - start
        key = rel >> 7
        slot = rel & 127
        acc = [jnp.zeros((TILE, 128), F32)] * ways
        top = [jnp.full((TILE, 128), -jnp.inf, F32)] * ways
        for c in range(width // 128):
            cols = slice(c * 128, (c + 1) * 128)
            w = c % ways
            logit = own_ref[rows, cols] + recv_ref[rows, cols]
            e_ref[rows, cols] = logit
            top[w] = jnp.maximum(top[w], logit)
            got = jnp.take_along_axis(logit, slot, axis=1, mode="promise_in_bounds")
            acc[w] = jnp.where(key == c, got, acc[w])
        hold[rows, :] = functools.reduce(jnp.maximum, top)
        picked = sum(acc)
        picks_ref[rows, :] = picked if first else picked + picks_in[rows, :]
        return carry

    def power(t, carry):
        rows = pl.ds(pl.multiple_of(t * TILE, TILE), TILE)
        top = stat_ref[rows, :]
        total = [jnp.zeros((TILE, 128), F32)] * ways
        for c in range(width // 128):
            cols = slice(c * 128, (c + 1) * 128)
            e = jnp.exp(e_ref[rows, cols] - top)
            e_ref[rows, cols] = e
            total[c % ways] += e
        hold[rows, :] = sum(total)
        return carry

    lax.fori_loop(0, half // TILE, pick, 0, unroll=8)
    stat_ref[...] = jnp.broadcast_to(jnp.max(hold[...], axis=1, keepdims=True), (half, 128))
    lax.fori_loop(0, half // TILE, power, 0, unroll=8)
    top = stat_ref[...]
    total = jnp.sum(hold[...], axis=1, keepdims=True)
    stat_ref[...] = jnp.where(lane == 0, top, total)
    if last:
        tops, totals = [top[:, 0:1]], [total]
        for ref in before:
            tops.append(ref[:, 0:1])
            totals.append(ref[:, 1:2])
        both = functools.reduce(jnp.maximum, tops)
        total = sum(s * jnp.exp(m - both) for m, s in zip(tops, totals))
        ids = ids_ref[...]
        inside = (ids >= 0) & (ids < start + width)
        picked = picks_ref[...] - both
        weight = jnp.where(inside, jnp.exp(picked), 0.0)
        mixed = jnp.sum(weight * (picked - lps_ref[...] + 1.0), axis=1, keepdims=True)
        plain = jnp.sum(weight, axis=1, keepdims=True)
        table = jnp.where(lane == 0, both, jnp.where(lane == 1, total, jnp.where(lane == 2, mixed, plain)))
        tot_ref[...] = table.T[:TILE, :]


def _exponentials(own, recv, chunks, index, terms, packed=None, rows=None, picks=None, before=(), kept=()):
    start, width = chunks[index]
    half = own.shape[0]
    first, last = index == 0, index == len(chunks) - 1
    table = pltpu.VMEM((half, 128), F32)
    args = [own, recv] + ([packed] if first else [*rows, picks]) + (list(before) if last else []) + list(kept)
    out = [pltpu.VMEM((half, width), F32), table, table]
    if first:
        out += [pltpu.VMEM((half, 128), jnp.int32), table]
    if last:
        out.append(pltpu.VMEM((TILE, half), F32))
    return _call(
        functools.partial(_exp_body, start, width, index, len(chunks), terms, len(kept)),
        "exponentials",
        args,
        out,
        _cost(8 * half * width, 12 * half * width),
        scratch=[pltpu.VMEM((half, 128), F32)],
    )


def _join_body(a_ref, b_ref, *refs):
    a, b = a_ref[...], b_ref[...]
    top = jnp.maximum(a[0:1], b[0:1])
    da, db = a[0:1] - top, b[0:1] - top
    fa, fb = jnp.exp(da), jnp.exp(db)
    total = a[1:2] * fa + b[1:2] * fb
    mixed = (a[2:3] + da * a[3:4]) * fa + (b[2:3] + db * b[3:4]) * fb
    plain = a[3:4] * fa + b[3:4] * fb
    refs[-1][...] = jnp.concatenate([top, total, mixed, plain, a[4:]], axis=0)


def _join_stats(a, b, kept):
    return _call(
        _join_body, "join_stats", [a, b, *kept], [pltpu.VMEM(a.shape, F32)], _cost(10 * a.size, 12 * a.size)
    )[0]


def _grad_body(chunks, terms, *refs):
    count = len(chunks)
    e_refs, stat_refs = refs[:count], refs[count : 2 * count]
    picks_ref, ids_ref, lps_ref, tot_ref = refs[2 * count : 2 * count + 4]
    g_ref, coef_ref, high_ref, low_ref = refs[-4:]
    half = tot_ref.shape[1]
    lanes = TILE * terms
    begin = chunks[0][0]
    width = sum(w for _, w in chunks)
    parts = (width + 255) // 256

    tot = jnp.concatenate([tot_ref[...], jnp.zeros((128 - TILE, half), F32)], axis=0).T
    top, total, mixed, plain, scale = (tot[:, i : i + 1] for i in range(5))
    log_sum = jnp.log(total)
    lse = top + log_sum
    sum_grad = scale * jnp.exp(-log_sum) * (mixed - log_sum * plain)
    for q, ref in enumerate(stat_refs):
        coef_ref[q] = jnp.broadcast_to(sum_grad * jnp.exp(ref[:, 0:1] - lse), (half, 128))
    rel = ids_ref[...] - begin
    inside = (rel >= 0) & (rel < width)
    support = picks_ref[...] - lse
    grad = scale * jnp.exp(support) * (support - lps_ref[...] + 1.0)
    grad = jnp.where(inside, grad, 0.0)
    high = grad.astype(BF16).astype(F32)
    high_ref[...] = high
    low_ref[...] = grad - high

    lane_row = lax.broadcasted_iota(jnp.int32, (TILE, lanes), 1) // terms
    mask = lane_row == lax.broadcasted_iota(jnp.int32, (TILE, lanes), 0)
    place = lax.broadcasted_iota(jnp.int32, (256, lanes), 0)

    def flat(x):
        return jnp.concatenate([x[:, :terms]] * TILE, axis=1)

    def tile(t):
        rows = pl.ds(pl.multiple_of(t * TILE, TILE), TILE)
        rel = flat(ids_ref[rows, :]) - begin
        key = jnp.where(mask, rel >> 8, -1)
        col = jnp.sum(jnp.where(mask, rel & 255, 0), axis=0, keepdims=True)
        high, low = flat(high_ref[rows, :]), flat(low_ref[rows, :])
        lhs = jnp.concatenate(
            [
                jnp.concatenate([jnp.where(key == c, high, 0.0), jnp.where(key == c, low, 0.0)], axis=1)
                for c in range(parts)
            ],
            axis=0,
        ).astype(BF16)
        hot = (place == jnp.broadcast_to(col, (256, lanes))).astype(F32).astype(BF16)
        rhs = jnp.concatenate([hot, hot], axis=1)
        return rows, lax.dot_general(lhs, rhs, NT, preferred_element_type=F32)

    def step(i, carry):
        pair = [tile(i * (STEP // TILE) + t) for t in range(STEP // TILE)]
        out_rows = pl.ds(pl.multiple_of(i * STEP, STEP), STEP)
        for q, (start, w) in enumerate(chunks):
            coefs = [coef_ref[q, rows, :] for rows, _ in pair]
            for at, size in _blocks(w, 128):
                col = start - begin + at
                c, off = col // 256, col % 256
                out = [
                    s[c * TILE : (c + 1) * TILE, off : off + size] - e_refs[q][rows, at : at + size] * coef
                    for (rows, s), coef in zip(pair, coefs)
                ]
                g_ref[out_rows, col : col + size] = jnp.concatenate(out, axis=0).astype(BF16)
        return carry

    lax.fori_loop(0, half // STEP, step, 0, unroll=4)


def _logit_grad(es, stats, picks, ids, lps, tot, chunks, terms):
    half = es[0].shape[0]
    width = sum(w for _, w in chunks)
    table = pltpu.VMEM((half, 128), F32)
    return _call(
        functools.partial(_grad_body, chunks, terms),
        "logit_grad",
        [*es, *stats, picks, ids, lps, tot],
        [pltpu.VMEM((half, width), BF16)],
        _cost(8 * half * width, 6 * half * width),
        scratch=[pltpu.VMEM((len(chunks), half, 128), F32), table, table],
    )


def _feature_body(start, count, own_ref, far_ref, w_ref, *refs):
    if count:
        before_ref, order_ref, keep_ref, send_ref, acc, other, weights, keep, send, sems, w_sems = refs
    else:
        acc, other, weights, sems, w_sems = refs
    blocks = _blocks(own_ref.shape[1], WIDE)
    fetches, copies = [], []
    for i, (at, size) in enumerate(blocks):
        cols = pl.ds(at, size)
        copies.append(pltpu.make_async_copy(far_ref.at[:, cols], other.at[:, cols], sems.at[i]))
        fetches.append(
            pltpu.make_async_copy(w_ref.at[:, pl.ds(start + at, size)], weights.at[:, cols], w_sems.at[i])
        )
        copies[i].start()
        fetches[i].start()
    for i, (at, size) in enumerate(blocks):
        cols = slice(at, at + size)
        copies[i].wait()
        grads = jnp.concatenate([own_ref[:, cols], other[:, cols]], axis=0)
        fetches[i].wait()
        part = lax.dot_general(grads, weights[:, cols], NT, preferred_element_type=F32)
        if i:
            acc[...] += part
        else:
            acc[...] = part + before_ref[...] if count else part
    if not count:
        return
    rows = acc.shape[0] // count
    block = [acc[pl.ds(pl.multiple_of(order_ref[d] * rows, rows), rows), :] for d in range(count)]
    send[...] = jnp.concatenate(block[1::2], axis=0).astype(BF16)
    copies = [pltpu.make_async_copy(send, send_ref, sems.at[0]), pltpu.make_async_copy(keep, keep_ref, w_sems.at[0])]
    copies[0].start()
    keep[...] = jnp.concatenate(block[::2], axis=0)
    copies[1].start()
    for copy in copies:
        copy.wait()


def _feature_terms(own, other, source, start, before=None, order=None):
    half, width = own.shape
    depth = source.shape[0]
    args = [own, other, source]
    specs = [LOCAL, REMOTE, REMOTE]
    count = len(_blocks(width, WIDE))
    scratch = [pltpu.VMEM((half, width), BF16), pltpu.VMEM((depth, width), BF16)]
    out, out_specs = [pltpu.VMEM((2 * half, depth), F32)], [LOCAL]
    if before is not None:
        args += [before, order]
        specs += [LOCAL, pl.BlockSpec(memory_space=pltpu.SMEM)]
        scratch = out + scratch + [pltpu.VMEM((half, depth), F32), pltpu.VMEM((half, depth), BF16)]
        out, out_specs = [pltpu.HBM((half, depth), F32), pltpu.HBM((half, depth), BF16)], [REMOTE] * 2
    return _call(
        functools.partial(_feature_body, start, 0 if before is None else order.shape[0]),
        "feature_terms",
        args,
        out,
        _cost(4 * half * depth * width, 2 * depth * width + 4 * half * width),
        specs=specs,
        out_specs=out_specs,
        scratch=scratch + [pltpu.SemaphoreType.DMA((count,)), pltpu.SemaphoreType.DMA((count,))],
        limit=20,
    )


def _weight_body(start, ht_ref, own_ref, far_ref, *refs):
    out_ref, ring, ht, other, sems, fetched = refs[-6:]
    blocks = _blocks(own_ref.shape[1], BLOCK)
    fetches = [pltpu.make_async_copy(ht_ref, ht, fetched.at[0])] + [
        pltpu.make_async_copy(far_ref.at[:, pl.ds(at, size)], other.at[:, pl.ds(at, size)], fetched.at[i + 1])
        for i, (at, size) in enumerate(blocks)
    ]
    for fetch in fetches:
        fetch.start()
    fetches[0].wait()
    copies = []
    for i, (at, size) in enumerate(blocks):
        slot = i % WRITES
        if i >= WRITES:
            copies[i - WRITES].wait()
        cols = slice(at, at + size)
        fetches[i + 1].wait()
        grads = jnp.concatenate([own_ref[:, cols], other[:, cols]], axis=0)
        ring[slot, :, :size] = jnp.dot(ht[...], grads, preferred_element_type=F32).astype(BF16)
        copy = pltpu.make_async_copy(
            ring.at[slot, :, pl.ds(0, size)], out_ref.at[:, pl.ds(start + at, size)], sems.at[slot]
        )
        copy.start()
        copies.append(copy)
    for copy in copies[-WRITES:]:
        copy.wait()


def _weight_grad(ht, own, other, start, width_all, before=None):
    depth, rows = ht.shape
    half, width = own.shape
    args = [ht, own, other]
    specs = [REMOTE, LOCAL, REMOTE]
    aliases = {}
    if before is not None:
        args.append(before)
        specs.append(pl.BlockSpec(memory_space=pl.ANY))
        aliases = {3: 0}
    return _call(
        functools.partial(_weight_body, start),
        "weight_grad",
        args,
        [jax.ShapeDtypeStruct((depth, width_all), BF16)],
        _cost(2 * rows * depth * width, 2 * depth * width + 2 * rows * width),
        specs=specs,
        out_specs=[pl.BlockSpec(memory_space=pl.ANY)],
        scratch=[
            pltpu.VMEM((WRITES, depth, BLOCK), BF16),
            pltpu.VMEM((depth, rows), BF16),
            pltpu.VMEM((half, width), BF16),
            pltpu.SemaphoreType.DMA((WRITES,)),
            pltpu.SemaphoreType.DMA((len(_blocks(width, BLOCK)) + 1,)),
        ],
        aliases=aliases,
        limit=16,
    )[0]


def per_device(hidden, head_weight, teacher_ids, teacher_logprobs, valid, row_weight):
    count = lax.axis_size("vocab")
    bits = count.bit_length() - 1
    r = lax.axis_index("row")
    v = lax.axis_index("vocab")
    width = head_weight.shape[1]
    half, own_terms = teacher_ids.shape
    terms = own_terms * count
    swap = [(0, 1), (1, 0)]
    chunks = _split(width, 4)
    groups = [[0, 1], [2, 3]]
    halves = [(sum(chunks[q][0] for q in group[:1]), sum(chunks[q][1] for q in group)) for group in groups]

    h = hidden[None]
    packed = None
    for b in reversed(range(bits)):
        perm = _xor(count, 1 << b)
        far = lax.ppermute(h, "vocab", perm)
        if packed is None:
            raw = (teacher_ids.T, teacher_logprobs.T)
            far_raw = tuple(lax.ppermute(x, "vocab", perm) for x in raw)
            far, far_raw = lax.optimization_barrier((far, far_raw))
            packed = jnp.stack([jnp.concatenate([x, y], axis=0).astype(F32) for x, y in zip(raw, far_raw)])
        else:
            far_packed = lax.ppermute(packed, "vocab", perm)
            if b == 0:
                _, source = lax.optimization_barrier((h, head_weight))
                fetched = _fetch(source, [chunks[q] for q in groups[0]])
                far, far_packed, fetched = lax.optimization_barrier((far, far_packed, fetched))
            else:
                far, far_packed = lax.optimization_barrier((far, far_packed))
            packed = jnp.concatenate([packed, far_packed], axis=1)
        bit = (v >> b) & 1
        first = bit == r if b == bits - 1 else bit == 0
        h = jnp.stack([jnp.where(first, h, far), jnp.where(first, far, h)], axis=1)
        h = h.reshape((-1,) + hidden.shape)
    h = h.reshape(-1, hidden.shape[1])
    packed = packed - jnp.array([1.0, 0.0], F32)[:, None, None] * (v * width).astype(F32)
    h, packed = lax.optimization_barrier((h, packed))

    def bring(*pieces):
        return head_weight, list(pieces)

    def swapped(x):
        return lax.ppermute(x, "row", swap)

    es, stats, parts, news = [], [], [], []
    for i in range(len(chunks)):
        if i in groups[0]:
            turn = i == 0
            own, send, *rest = _partial_logits(h, fetched[i : i + 1], turn, bring(chunks[i + len(groups[0])]))
            news.append(rest[-1])
            if turn:
                ht = rest[0]
        else:
            own, send = _partial_logits(h, [news[i - len(groups[0])]])
        parts.append((own, swapped(send)))
    picks = rows = None
    for i, (own, recv) in enumerate(parts):
        e, picks, stat, *rest = _exponentials(
            own, recv, chunks, i, terms, packed=packed, rows=rows, picks=picks, before=stats, kept=es
        )
        if i == 0:
            rows = rest
        es.append(e)
        stats.append(stat)
    ids, lps = rows

    scale = row_weight * valid.astype(F32)
    joined = jnp.concatenate([rest[0][:4], scale[None], jnp.zeros((3, half), F32)], axis=0)
    for b in range(bits):
        far = lax.ppermute(joined, "vocab", _xor(count, 1 << b))
        joined = _join_stats(joined, far, [*es, *stats, picks, ids, lps])

    grads = []
    for group in groups:
        (own,) = _logit_grad(
            [es[q] for q in group],
            [stats[q] for q in group],
            picks,
            ids,
            lps,
            joined,
            [chunks[q] for q in group],
            terms,
        )
        grads.append((own, swapped(own)))

    order = (jnp.arange(count, dtype=jnp.int32) ^ v) ^ (r * (count // 2))
    starts = [start for start, _ in halves]
    (before,) = _feature_terms(*grads[0], head_weight, starts[0])
    keep, send = _feature_terms(*grads[1], head_weight, starts[1], before, order)

    far = lax.ppermute(send, "vocab", _xor(count, 1))
    weight_grad = _weight_grad(ht, *grads[0], starts[0], width)
    keep = keep + far.astype(F32)
    keep = keep.reshape((count // 2,) + hidden.shape)
    total = keep[0]
    for d in range(1, count // 2):
        far = lax.ppermute(keep[d].astype(BF16), "vocab", _xor(count, 2 * d))
        total = total + far.astype(F32)
    hidden_grad = total.astype(BF16)

    weight_grad = _weight_grad(ht, *grads[1], starts[1], width, weight_grad)
    return hidden_grad, weight_grad


def solution(mesh):
    return jax.shard_map(
        per_device,
        mesh=mesh,
        in_specs=(
            P(("grp", "vocab"), "row"),
            P("row", "vocab"),
            P(("grp", "row"), "vocab"),
            P(("grp", "row"), "vocab"),
            P(("grp", "row")),
            P(("grp", "row")),
        ),
        out_specs=(P(("grp", "vocab"), "row"), P(("grp", "row"), "vocab")),
        check_vma=False,
    )
```
